512 devices in a mesh: pairs: 64 (over x, z, core), virt: 8 (over y).
Axes of the slice: x: 4, y: 8, z: 8, core: 2. Of those that a mesh axis runs over, the one named last changes fastest.
Arguments:
- amplitudes: bfloat16 [1024, 384, 384], P(('pairs', 'virt')), may hold values from -6 to 6
- factors: bfloat16 [2, 32, 128, 4096], P(None, None, 'virt', 'pairs'), may hold values from -0.21875 to 0.21875
- tiles: int32 [1024, 3], P('pairs'), may hold values from 0 to 31, as said below
- mirror: int32 [1024], P(('pairs', 'virt')), may hold values from 0 to 1023, as said below
- pair_energy: float32 [1024], P(('pairs', 'virt')), may hold values from -3 to -0.5
- virt_energy: float32 [4096], replicated, may hold values from 0.5 to 3
Outputs:
- residual: float32 [1024, 384, 384], P(('pairs', 'virt'))
- updated: bfloat16 [1024, 384, 384], P(('pairs', 'virt'))
The draws below stay inside these ranges and needn't reach their ends.
Inputs may be any that keep to these rules, and one draw needn't show every extreme that they name: Each row names 3 different tiles; a pair and its mirror name the same tiles in the same order. mirror is an involution without fixed points; the mirror of a pair on a device lies on the device with the same index of virt and the index of pairs half the pairs axis away.
All inputs are finite; a program needn't handle non-finite values.
Results may differ from the reference program's by a relative error of at most 0.005.
Values may be sent and summed in bfloat16 or wider, within the bound.
No kernel may reach another device: no remote copies, remote signals or barrier semaphores. Data moves between devices by JAX's collectives and lax.ppermute only.
A program may use at most 128 MiB of HBM per device.

```python
import jax
import jax.numpy as jnp
from jax import lax

V = 128
K = 3
NT = 32
NQ = 2
PAIR_DEV = 2
NV = 4096
NP = 1024


def pairing(key):
    blocks = NP // PAIR_DEV
    half_blocks = blocks // 2
    slot_keys = jax.random.split(jax.random.fold_in(key, 11), half_blocks)
    shuffle = jax.vmap(lambda k: jax.random.permutation(k, PAIR_DEV))(slot_keys).astype(jnp.int32)
    inverse = jnp.argsort(shuffle, axis=1).astype(jnp.int32)
    tile_keys = jax.random.split(jax.random.fold_in(key, 12), half_blocks * PAIR_DEV)
    lower_tiles = jax.vmap(lambda k: jax.random.permutation(k, NT)[:K])(tile_keys).astype(jnp.int32)
    lower_tiles = lower_tiles.reshape(half_blocks, PAIR_DEV, K)
    block_ids = jnp.arange(half_blocks, dtype=jnp.int32)[:, None]
    lower_mirror = (block_ids + half_blocks) * PAIR_DEV + shuffle
    upper_mirror = block_ids * PAIR_DEV + inverse
    upper_tiles = jnp.take_along_axis(lower_tiles, inverse[:, :, None], axis=1)
    mirror_all = jnp.concatenate([lower_mirror, upper_mirror], axis=0).reshape(NP)
    tiles_all = jnp.concatenate([lower_tiles, upper_tiles], axis=0).reshape(NP, K)
    return (tiles_all.astype(jnp.int32), mirror_all.astype(jnp.int32))


def draw_tiles(key, part):
    tiles_all, mirror_all = pairing(key)
    return tiles_all


def draw_mirror(key, part):
    tiles_all, mirror_all = pairing(key)
    return mirror_all


def block_levels(own_key, shape, shards, low, largest):
    def one(position, parts):
        draws = jax.random.uniform(jax.random.fold_in(jax.random.fold_in(own_key, 6), position), (parts,), jnp.float32, low / len(shards), largest / len(shards))
        return jnp.repeat(jnp.exp(draws), shape[position] // parts).reshape((-1,) + (1,) * (len(shape) - position - 1))

    factor_of = one(*shards[0])
    for cut in shards[1:]:
        factor_of = factor_of * one(*cut)
    return factor_of


def normal_values(stream_key, extent, width, bound, shards=(), held_as=jnp.bfloat16):
    entries = jax.random.normal(stream_key, extent, jnp.float32) * width
    if len(shards) > 0:
        entries = block_levels(stream_key, extent, shards, -0.22, 0.18) * entries
    return jnp.clip(entries, min=-bound, max=bound).astype(held_as)


def setup_inputs(seed: int = 0) -> dict:
    streams_of = jax.random.split(jax.random.key(seed), 7)
    amplitudes = normal_values(streams_of[0], (NP, K * V, K * V), 1.0, 6.0, ((0, 512),))
    factors = normal_values(streams_of[1], (NQ, NT, V, NV), (2 * K * V) ** -0.5, 0.21875, ((2, 8), (3, 64)))
    tiles = draw_tiles(jax.random.fold_in(streams_of[6], 71), 0)
    mirror = draw_mirror(jax.random.fold_in(streams_of[6], 71), 0)
    pair_energy = jnp.clip(-3.0 + 2.5 * jax.random.uniform(streams_of[4], (NP,), jnp.float32) ** block_levels(streams_of[4], (NP,), ((0, 512),), -0.2, 0.2), -3.0, -0.5)
    virt_energy = jnp.clip(jax.random.uniform(streams_of[5], (NV,), jnp.float32, 0.5, 3.0), 0.5, 3.0)
    return dict(amplitudes=amplitudes, factors=factors, tiles=tiles, mirror=mirror, pair_energy=pair_energy, virt_energy=virt_energy)


def reference(amplitudes, factors, tiles, mirror, pair_energy, virt_energy):
    offsets = jnp.arange(V, dtype=jnp.int32)
    rows_index = (tiles[:, :, None] * V + offsets[None, None, :]).reshape(NP, K * V).astype(jnp.int32)
    square_factors = factors.reshape(NQ, NV, NV)

    def one_pair(pair_item):
        pair_index, pair_amps = pair_item
        domain = square_factors[:, pair_index][:, :, pair_index]
        half_ladder = jnp.einsum("qxy,yz->qxz", domain.astype(jnp.float32), pair_amps.astype(jnp.float32)).astype(jnp.bfloat16)
        return jnp.einsum("qxz,qwz->xw", half_ladder.astype(jnp.float32), domain.astype(jnp.float32))

    ladder = lax.map(one_pair, (rows_index, amplitudes))
    residual = ladder + jnp.swapaxes(ladder[mirror], 1, 2)
    energies = virt_energy[rows_index]
    denominators = energies[:, :, None] + energies[:, None, :] - pair_energy[:, None, None]
    updated = (amplitudes.astype(jnp.float32) - residual / denominators).astype(jnp.bfloat16)
    return residual, updated
```

```python
import functools

import jax
import jax.numpy as jnp
from jax import lax
from jax.experimental import pallas as pl
from jax.experimental.pallas import tpu as pltpu
from jax.sharding import Mesh, PartitionSpec as P

V = 128
K = 3
NX, NZ, NC, NY = 4, 8, 2, 8
NT = 32
NQ = 2
HALF = V // 2
GROUP = 16
WIDTH = K * V
SOURCES = NX * NZ * NC
PLANE = NZ * NC * NY
MSG1 = NT + 2
MSG2 = 2 * K * K
SMEM = pltpu.MemorySpace.SMEM
VMEM = pltpu.MemorySpace.VMEM
PARAMS = pltpu.CompilerParams(vmem_limit_bytes=24 * 1024 * 1024)


def spread_kernel(tiles_ref, factors_ref, out_ref, wide, staged):
    wide[...] = factors_ref[...].astype(jnp.float32).reshape(NQ * NT * 16, HALF)
    lane = lax.broadcasted_iota(jnp.int32, (2, V), 1)
    tile_row = jnp.zeros((2, V), jnp.float32)
    for member in range(GROUP):
        for k in range(K):
            tile_row = jnp.where(
                lane == member * K + k, tiles_ref[k, member].astype(jnp.float32), tile_row
            )
    for z in range(NZ):
        for q in range(NQ):
            base = (z * NQ + q) * MSG1
            for part in range(NT // 8):
                first = (q * NT + part * 8) * 16 + z
                upper = wide[pl.ds(first, 8, stride=16), :]
                lower = wide[pl.ds(first + 8, 8, stride=16), :]
                staged[pl.ds(base + part * 8, 8), :] = jnp.concatenate([upper, lower], axis=1)
            staged[pl.ds(base + NT, 2), :] = tile_row
    packed = staged[...].astype(jnp.bfloat16)
    for x in range(NX):
        out_ref[x] = packed


def select_kernel(info_ref, held_ref, out_ref, wide, staged, tile_rows, tiles, sem):
    wide[...] = held_ref[...].astype(jnp.float32)
    first = info_ref[0] * (GROUP * MSG1) + NT
    for group in range(GROUP):
        tile_rows[pl.ds(group, 1), :] = wide[pl.ds(first + group * MSG1, 1), :].astype(jnp.int32)
    copy = pltpu.make_async_copy(tile_rows, tiles, sem)
    copy.start()
    copy.wait()
    offset = info_ref[1] * K

    def one_group(group, carry):
        for y in range(NY):
            named = [tiles[group, offset + 2 * K * y + k] for k in range(K)]
            base = group * (NY * MSG2) + y * MSG2
            for l in range(K):
                strip = named[l] * (2 * MSG1)
                for k in range(K):
                    row = strip + named[k]
                    for h in range(2):
                        staged[pl.ds(base + (l * 2 + h) * K + k, 1), :] = wide[
                            pl.ds(row + h * MSG1, 1), :
                        ]
        return carry

    lax.fori_loop(0, GROUP, one_group, 0)
    out_ref[...] = staged[...].astype(jnp.bfloat16)


def ladder_kernel(info_ref, amps_ref, mirror_amps_ref, blocks_ref, ladder_ref, sent_ref, wide, domain):
    wide[...] = blocks_ref[...].astype(jnp.float32)
    left = lax.broadcasted_iota(jnp.int32, (NZ, V), 1) < HALF
    for q in range(NQ):
        for y in range(NY):
            for l in range(K):
                for k in range(K):
                    first = (q * NY + y) * MSG2 + l * 2 * K + k
                    stride = NC * NY * MSG2
                    here = wide[pl.ds(first, NZ, stride=stride), :]
                    there = wide[pl.ds(first + K, NZ, stride=stride), :]
                    upper = jnp.where(left, here, pltpu.roll(there, HALF, 1))
                    lower = jnp.where(left, pltpu.roll(here, HALF, 1), there)
                    domain[q, pl.ds(k * V + y * 16, 16), pl.ds(l * V, V)] = jnp.concatenate(
                        [upper, lower], axis=0
                    ).astype(jnp.bfloat16)
    own = amps_ref[info_ref[2]]
    mirrored = mirror_amps_ref[...]
    total = jnp.zeros((WIDTH, WIDTH), jnp.float32)
    across = (((1,), (1,)), ((), ()))
    for q in range(NQ):
        part = domain[q]
        half = jnp.dot(part, own, preferred_element_type=jnp.float32)
        half = half + lax.dot_general(part, mirrored, across, preferred_element_type=jnp.float32)
        total = total + lax.dot_general(
            half.astype(jnp.bfloat16), part, across, preferred_element_type=jnp.float32
        )
    ladder_ref[...] = total
    sent_ref[...] = total.astype(jnp.bfloat16)


def update_block(info_ref, tiles_ref, pair_energy_ref, energy_ref, slot, residual, amps_ref, residual_ref, updated_ref):
    member = 2 * info_ref[3] + slot
    step = pl.program_id(0)
    across = jnp.concatenate([energy_ref[pl.ds(tiles_ref[k, member], 1), :] for k in range(K)], axis=1)
    down = energy_ref[pl.ds(tiles_ref[step, member], 1), :]
    down = jnp.transpose(jnp.broadcast_to(down, (V, V)))
    down = jnp.concatenate([down] * K, axis=1)
    denominators = down + across - pair_energy_ref[slot]
    residual_ref[0] = residual
    updated_ref[0] = (amps_ref[0].astype(jnp.float32) - residual / denominators).astype(jnp.bfloat16)


def own_kernel(info_ref, tiles_ref, pair_energy_ref, energy_ref, ladder_ref, amps_ref, residual_ref, updated_ref):
    update_block(
        info_ref, tiles_ref, pair_energy_ref, energy_ref, info_ref[2], ladder_ref[...],
        amps_ref, residual_ref, updated_ref,
    )


def other_kernel(
    info_ref, tiles_ref, pair_energy_ref, energy_ref, ladder_ref, amps_ref, res_in, upd_in, residual_ref, updated_ref
):
    update_block(
        info_ref, tiles_ref, pair_energy_ref, energy_ref, 1 - info_ref[2],
        jnp.transpose(ladder_ref[...].astype(jnp.float32)), amps_ref, residual_ref, updated_ref,
    )


def whole(space=VMEM):
    return pl.BlockSpec(memory_space=space)


def shards(amplitudes, factors, tiles, mirror, pair_energy, virt_energy):
    f32, bf16 = jnp.float32, jnp.bfloat16
    x = lax.axis_index("x")
    sel = jnp.where(x < NX // 2, 0, 1 - mirror[0] % 2)
    info = jnp.stack([x % (NX // 2), x // (NX // 2), sel, lax.axis_index("y")]).astype(jnp.int32)
    tiles_t = tiles.T

    spread = pl.pallas_call(
        spread_kernel,
        out_shape=jax.ShapeDtypeStruct((NX, NZ * NC * MSG1, V), bf16),
        in_specs=[whole(SMEM), whole()],
        out_specs=whole(),
        scratch_shapes=[pltpu.VMEM((NQ * NT * 16, HALF), f32), pltpu.VMEM((NZ * NC * MSG1, V), f32)],
        compiler_params=PARAMS,
        name="spread",
    )(tiles_t, factors)
    held = lax.all_to_all(
        spread.reshape(SOURCES, MSG1 // 2, 2, V), ("x", "z", "c"), 0, 0, tiled=True
    )
    going = lax.dynamic_index_in_dim(amplitudes, 1 - sel, 0, keepdims=False)
    opposite = [((i + NX // 2) % NX, i) for i in range(NX)]
    mirror_amps = lax.ppermute(going, "x", opposite)

    selected = pl.pallas_call(
        select_kernel,
        out_shape=jax.ShapeDtypeStruct((PLANE * MSG2, V), bf16),
        in_specs=[whole(SMEM), whole()],
        out_specs=whole(),
        scratch_shapes=[
            pltpu.VMEM((SOURCES * MSG1, V), f32),
            pltpu.VMEM((PLANE * MSG2, V), f32),
            pltpu.VMEM((GROUP, V), jnp.int32),
            pltpu.SMEM((GROUP, V), jnp.int32),
            pltpu.SemaphoreType.DMA,
        ],
        compiler_params=PARAMS,
        name="select",
    )(info, held.reshape(SOURCES * MSG1, V))
    blocks = lax.all_to_all(
        selected.reshape(PLANE, MSG2 // 2, 2, V), ("z", "c", "y"), 0, 0, tiled=True
    )

    ladder, sent = pl.pallas_call(
        ladder_kernel,
        out_shape=(
            jax.ShapeDtypeStruct((WIDTH, WIDTH), f32),
            jax.ShapeDtypeStruct((WIDTH, WIDTH), bf16),
        ),
        in_specs=[whole(SMEM), whole(), whole(), whole()],
        out_specs=(whole(), whole()),
        scratch_shapes=[pltpu.VMEM((PLANE * MSG2, V), f32), pltpu.VMEM((NQ, WIDTH, WIDTH), bf16)],
        compiler_params=PARAMS,
        name="ladder",
    )(info, amplitudes, mirror_amps, blocks.reshape(PLANE * MSG2, V))
    received = lax.ppermute(sent, "x", opposite)

    energies = virt_energy.reshape(NT, V)
    outs = (
        jax.ShapeDtypeStruct(amplitudes.shape, f32),
        jax.ShapeDtypeStruct(amplitudes.shape, bf16),
    )

    def band(pick):
        return pl.BlockSpec((1, V, WIDTH), lambda i, info_ref: (pick(info_ref[2]), i, 0))

    def common(body, pick, ladder_spec, extra):
        return pl.pallas_call(
            body,
            out_shape=outs,
            grid_spec=pltpu.PrefetchScalarGridSpec(
                num_scalar_prefetch=1,
                grid=(K,),
                in_specs=[whole(SMEM), whole(SMEM), pl.BlockSpec((NT, V), lambda i, info_ref: (0, 0)), ladder_spec, band(pick)]
                + extra,
                out_specs=(band(pick), band(pick)),
            ),
            input_output_aliases={6: 0, 7: 1} if extra else {},
            cost_estimate=pl.CostEstimate(flops=3 * WIDTH * WIDTH, bytes_accessed=10 * WIDTH * WIDTH, transcendentals=0),
            compiler_params=PARAMS,
            name="own" if not extra else "other",
        )

    residual, updated = common(
        own_kernel, lambda s: s, pl.BlockSpec((V, WIDTH), lambda i, info_ref: (i, 0)), []
    )(info, tiles_t, pair_energy, energies, ladder, amplitudes)
    residual, updated = common(
        other_kernel,
        lambda s: 1 - s,
        pl.BlockSpec((WIDTH, V), lambda i, info_ref: (0, i)),
        [whole(pl.ANY), whole(pl.ANY)],
    )(info, tiles_t, pair_energy, energies, received, amplitudes, residual, updated)
    return (residual, updated)


def solution(mesh):
    fine = Mesh(mesh.devices.reshape(NX, NZ, NC, NY), ("x", "z", "c", "y"))
    pairs = ("x", "z", "c")
    return jax.shard_map(
        shards,
        mesh=fine,
        in_specs=(
            P(pairs + ("y",), None, None),
            P(None, None, "y", pairs),
            P(pairs, None),
            P(pairs + ("y",)),
            P(pairs + ("y",)),
            P(),
        ),
        out_specs=(P(pairs + ("y",), None, None), P(pairs + ("y",), None, None)),
        check_vma=False,
    )
```

```python
import jax
import jax.numpy as jnp
from jax import lax
from jax.experimental import pallas as pl
from jax.experimental.pallas import tpu as pltpu
from jax.sharding import Mesh, PartitionSpec as P

V = 128
K = 3
NX, NU, NB, NC, NY = 4, 2, 4, 2, 8
NT = 32
NQ = 2
HALF = V // 2
GROUP = 16
WIDTH = K * V
ROWS = NX * NB
SOURCES = NU * ROWS
PLANE = ROWS * NY
MSG1 = NT + 2
HELD = SOURCES * MSG1
MSG2 = 2 * K * K
SMEM = pltpu.MemorySpace.SMEM
VMEM = pltpu.MemorySpace.VMEM
PARAMS = pltpu.CompilerParams(vmem_limit_bytes=24 * 1024 * 1024)


def spread_kernel(tiles_hbm, factors_hbm, out_ref, tiles, raw, wide, staged, sems):
    copies = [pltpu.make_async_copy(tiles_hbm, tiles, sems.at[0])]
    part = NT // 2
    for i in range(2):
        strip = pl.ds(i * part, part)
        copies.append(pltpu.make_async_copy(factors_hbm.at[:, strip], raw.at[:, strip], sems.at[1 + i]))
    for copy in copies:
        copy.start()
    copies[0].wait()
    lane = lax.broadcasted_iota(jnp.int32, (2, V), 1)
    tile_row = jnp.zeros((2, V), jnp.float32)
    for member in range(GROUP):
        for k in range(K):
            tile_row = jnp.where(lane == member * K + k, tiles[k, member].astype(jnp.float32), tile_row)
    for row in range(ROWS):
        staged[pl.ds(row * MSG1 + NT, 2), :] = tile_row
    for i in range(2):
        copies[1 + i].wait()
        for q in range(NQ):
            first = (q * NT + i * part) * ROWS
            wide[pl.ds(first, part * ROWS), :] = (
                raw[q, pl.ds(i * part, part)].astype(jnp.float32).reshape(part * ROWS, HALF)
            )
        for row in range(ROWS):
            for eight in range(part // 8):
                first = (i * part + eight * 8) * ROWS + row
                sides = [wide[pl.ds(q * NT * ROWS + first, 8, stride=ROWS), :] for q in range(NQ)]
                staged[pl.ds(row * MSG1 + i * part + eight * 8, 8), :] = jnp.concatenate(sides, axis=1)
    packed = staged[...].astype(jnp.bfloat16)
    for u in range(NU):
        out_ref[u] = packed


def select_kernel(info_ref, mine_ref, theirs_ref, out_ref, wide, staged, tile_rows, tiles, sem):
    slab = ROWS * MSG1
    core = info_ref[1]
    start = pl.multiple_of(info_ref[0] * slab, 16)
    wide[pl.ds(core, HELD, stride=2), :] = mine_ref[...].astype(jnp.float32)
    first = 2 * (start + NT) + core
    for group in range(GROUP // 2):
        named = wide[pl.ds(first + 2 * group * MSG1, 1), :].astype(jnp.int32)
        tile_rows[pl.ds(group, 1), :] = 2 * named
        place = ((named >> 2) & 1) * ROWS + (named >> 3) * NB + (named & (NB - 1))
        tile_rows[pl.ds(GROUP // 2 + group, 1), :] = 2 * MSG1 * place
    copy = pltpu.make_async_copy(tile_rows, tiles, sem)
    copy.start()
    wide[pl.ds(1 - core, HELD, stride=2), :] = theirs_ref[...].astype(jnp.float32)
    copy.wait()

    def one_group(group, carry):
        for parity in range(2):
            for y in range(NY):
                lanes = [(2 * y + parity) * K + k for k in range(K)]
                named = [tiles[group, lane] for lane in lanes]
                strips = [tiles[GROUP // 2 + group, lane] for lane in lanes]
                base = group * MSG2 + (y * ROWS + parity * (GROUP // 2)) * MSG2
                for l in range(K):
                    for k in range(K):
                        staged[pl.ds(base + (l * K + k) * 2, 2), :] = wide[
                            pl.ds(pl.multiple_of(strips[l] + named[k], 2), 2), :
                        ]
        return carry

    lax.fori_loop(0, GROUP // 2, one_group, 0)
    out_ref[...] = staged[...].astype(jnp.bfloat16)


ACROSS = (((1,), (1,)), ((), ()))


def ladder_kernel(info_ref, amps_ref, mirror_amps_ref, blocks_ref, sent_ref, domain, half, mirror_half, wide):
    wide[...] = blocks_ref[...].astype(jnp.float32)
    left = lax.broadcasted_iota(jnp.int32, (ROWS, V), 1) < HALF
    for y in range(NY):
        for l in range(K):
            for k in range(K):
                first = y * ROWS * MSG2 + (l * K + k) * 2
                sides = [wide[pl.ds(first + h, ROWS, stride=MSG2), :] for h in range(2)]
                rows = pl.ds(k * V + y * ROWS, ROWS)
                for q in range(NQ):
                    block = jnp.where(
                        left,
                        sides[0] if q == 0 else pltpu.roll(sides[0], HALF, 1),
                        sides[1] if q == 1 else pltpu.roll(sides[1], HALF, 1),
                    )
                    domain[rows, pl.ds(q * WIDTH + l * V, V)] = block.astype(jnp.bfloat16)
    own = amps_ref[info_ref[2]]
    mirrored = mirror_amps_ref[...]
    for q in range(NQ):
        columns = pl.ds(q * WIDTH, WIDTH)
        part = domain[:, columns]
        half[:, columns] = jnp.dot(part, own, preferred_element_type=jnp.float32).astype(jnp.bfloat16)
        mirror_half[:, columns] = jnp.dot(part, mirrored, preferred_element_type=jnp.float32).astype(
            jnp.bfloat16
        )
    sent_ref[...] = (
        lax.dot_general(domain[...], half[...], ACROSS, preferred_element_type=jnp.float32)
        + lax.dot_general(mirror_half[...], domain[...], ACROSS, preferred_element_type=jnp.float32)
    ).astype(jnp.bfloat16)


def denominators_of(info_ref, tiles_ref, pair_energy_ref, energy_ref, slot):
    member = 2 * info_ref[3] + slot
    rows = [energy_ref[pl.ds(tiles_ref[k, member], 1), :] for k in range(K)]
    across = jnp.concatenate(rows, axis=1)
    bands = []
    for row in rows:
        down = jnp.transpose(jnp.broadcast_to(row, (V, V)))
        bands.append(jnp.concatenate([down] * K, axis=1) + across - pair_energy_ref[slot])
    return bands


def write_pair(slot, denominator_of, residual_of, amps_ref, residual_out, updated_out, residual_buf, updated_buf, sems):
    copies = []
    for step in range(K):
        band = pl.ds(step * V, V)
        residual = residual_of(band)
        residual_buf[band, :] = residual
        updated_buf[band, :] = (
            amps_ref[slot, band, :].astype(jnp.float32) - residual / denominator_of(step)
        ).astype(jnp.bfloat16)
        for buf, out, sem in (
            (residual_buf, residual_out, sems.at[0, step]),
            (updated_buf, updated_out, sems.at[1, step]),
        ):
            copy = pltpu.make_async_copy(buf.at[band, :], out.at[slot, band, :], sem)
            copy.start()
            copies.append(copy)
    for copy in copies:
        copy.wait()


def own_kernel(
    info_ref, tiles_ref, pair_energy_ref, energy_ref, amps_ref, domain, half, mirror_half,
    residual_out, updated_out, other_ref, residual_buf, updated_buf, sems,
):
    energies = (info_ref, tiles_ref, pair_energy_ref, energy_ref)
    slot = info_ref[2]
    for step, band in enumerate(denominators_of(*energies, 1 - slot)):
        other_ref[pl.ds(step * V, V), :] = band
    bands = denominators_of(*energies, slot)

    def residual_of(band):
        return lax.dot_general(
            half[band, :], domain[...], ACROSS, preferred_element_type=jnp.float32
        ) + lax.dot_general(domain[band, :], mirror_half[...], ACROSS, preferred_element_type=jnp.float32)

    write_pair(
        slot, lambda step: bands[step], residual_of, amps_ref,
        residual_out, updated_out, residual_buf, updated_buf, sems,
    )


def other_kernel(
    info_ref, amps_ref, received_ref, denominators_ref, residual_in, updated_in,
    residual_out, updated_out, residual_buf, updated_buf, sems,
):
    write_pair(
        1 - info_ref[2],
        lambda step: denominators_ref[pl.ds(step * V, V), :],
        lambda band: received_ref[band, :].astype(jnp.float32),
        amps_ref, residual_out, updated_out, residual_buf, updated_buf, sems,
    )


def whole(space=VMEM):
    return pl.BlockSpec(memory_space=space)


def shards(amplitudes, factors, tiles, mirror, pair_energy, virt_energy):
    f32, bf16 = jnp.float32, jnp.bfloat16
    x = lax.axis_index("x")
    sel = jnp.where(x < NX // 2, 0, 1 - (mirror[0] & 1))
    info = jnp.stack([lax.axis_index(a) for a in ("u", "c")] + [sel, lax.axis_index("y")]).astype(jnp.int32)
    tiles_t = tiles.T

    spread = pl.pallas_call(
        spread_kernel,
        out_shape=jax.ShapeDtypeStruct((NU, ROWS * MSG1, V), bf16),
        in_specs=[whole(pltpu.MemorySpace.HBM), whole(pltpu.MemorySpace.HBM)],
        out_specs=whole(),
        scratch_shapes=[
            pltpu.SMEM(tiles_t.shape, jnp.int32),
            pltpu.VMEM(factors.shape, bf16),
            pltpu.VMEM((NQ * NT * ROWS, HALF), f32),
            pltpu.VMEM((ROWS * MSG1, V), f32),
            pltpu.SemaphoreType.DMA((3,)),
        ],
        compiler_params=pltpu.CompilerParams(vmem_limit_bytes=60 * 1024 * 1024),
        name="spread",
    )(tiles_t, factors)
    held = lax.all_to_all(spread.reshape(SOURCES, MSG1 // 2, 2, V), ("u", "x", "b"), 0, 0, tiled=True)
    theirs = lax.ppermute(held, "c", [(1, 0), (0, 1)])
    going = lax.dynamic_index_in_dim(amplitudes, 1 - sel, 0, keepdims=False)
    opposite = [((i + NX // 2) % NX, i) for i in range(NX)]
    mirror_amps = lax.ppermute(going, "x", opposite)

    selected = pl.pallas_call(
        select_kernel,
        out_shape=jax.ShapeDtypeStruct((PLANE * MSG2, V), bf16),
        in_specs=[whole(SMEM), whole(), whole()],
        out_specs=whole(),
        scratch_shapes=[
            pltpu.VMEM((NC * HELD, V), f32),
            pltpu.VMEM((PLANE * MSG2, V), f32),
            pltpu.VMEM((GROUP, V), jnp.int32),
            pltpu.SMEM((GROUP, V), jnp.int32),
            pltpu.SemaphoreType.DMA,
        ],
        compiler_params=PARAMS,
        name="select",
    )(info, held.reshape(HELD, V), theirs.reshape(HELD, V))
    blocks = lax.all_to_all(
        selected.reshape(PLANE, MSG2 // 2, 2, V), ("y", "x", "b"), 0, 0, tiled=True
    )

    wide_half = jax.ShapeDtypeStruct((WIDTH, NQ * WIDTH), bf16)
    sent, domain, half, mirror_half = pl.pallas_call(
        ladder_kernel,
        out_shape=(jax.ShapeDtypeStruct((WIDTH, WIDTH), bf16), wide_half, wide_half, wide_half),
        in_specs=[whole(SMEM), whole(), whole(), whole()],
        out_specs=(whole(),) * 4,
        scratch_shapes=[pltpu.VMEM((PLANE * MSG2, V), f32)],
        compiler_params=PARAMS,
        name="ladder",
    )(info, amplitudes, mirror_amps, blocks.reshape(PLANE * MSG2, V))
    received = lax.ppermute(sent, "x", opposite)

    energies = virt_energy.reshape(NT, V)
    outs = (
        jax.ShapeDtypeStruct(amplitudes.shape, f32),
        jax.ShapeDtypeStruct(amplitudes.shape, bf16),
    )
    buffers = [
        pltpu.VMEM((WIDTH, WIDTH), f32),
        pltpu.VMEM((WIDTH, WIDTH), bf16),
        pltpu.SemaphoreType.DMA((2, K)),
    ]
    residual, updated, denominators = pl.pallas_call(
        own_kernel,
        out_shape=outs + (jax.ShapeDtypeStruct((WIDTH, WIDTH), f32),),
        in_specs=[whole(SMEM)] * 3 + [whole()] * 5,
        out_specs=(whole(pl.ANY), whole(pl.ANY), whole()),
        scratch_shapes=buffers,
        cost_estimate=pl.CostEstimate(flops=8 * WIDTH**3, bytes_accessed=10 * WIDTH**2, transcendentals=0),
        compiler_params=PARAMS,
        name="own",
    )(info, tiles_t, pair_energy, energies, amplitudes, domain, half, mirror_half)
    residual, updated = pl.pallas_call(
        other_kernel,
        out_shape=outs,
        in_specs=[whole(SMEM), whole(), whole(), whole(), whole(pl.ANY), whole(pl.ANY)],
        out_specs=(whole(pl.ANY),) * 2,
        scratch_shapes=buffers,
        input_output_aliases={4: 0, 5: 1},
        cost_estimate=pl.CostEstimate(flops=4 * WIDTH**2, bytes_accessed=10 * WIDTH**2, transcendentals=0),
        compiler_params=PARAMS,
        name="other",
    )(info, amplitudes, received, denominators, residual, updated)
    return (residual, updated)


def solution(mesh):
    fine = Mesh(mesh.devices.reshape(NX, NU, NB, NC, NY), ("x", "u", "b", "c", "y"))
    pairs = ("x", "u", "b", "c")
    return jax.shard_map(
        shards,
        mesh=fine,
        in_specs=(
            P(pairs + ("y",), None, None),
            P(None, None, "y", pairs),
            P(pairs, None),
            P(pairs + ("y",)),
            P(pairs + ("y",)),
            P(),
        ),
        out_specs=(P(pairs + ("y",), None, None), P(pairs + ("y",), None, None)),
        check_vma=False,
    )
```

```python
import jax
import jax.numpy as jnp
from jax import lax
from jax.experimental import pallas as pl
from jax.experimental.pallas import tpu as pltpu
from jax.sharding import Mesh, PartitionSpec as P

V = 128
K = 3
NX, NU, NB, NC, NY = 4, 2, 4, 2, 8
NT = 32
NQ = 2
HALF = V // 2
GROUP = 16
WIDTH = K * V
ROWS = NX * NB
SOURCES = NU * ROWS
PLANE = ROWS * NY
MSG1 = NT + 2
HELD = SOURCES * MSG1
MSG2 = 2 * K * K
SMEM = pltpu.MemorySpace.SMEM
VMEM = pltpu.MemorySpace.VMEM
PARAMS = pltpu.CompilerParams(vmem_limit_bytes=24 * 1024 * 1024)


def spread_kernel(tiles_hbm, factors_hbm, out_ref, tiles, raw, wide, staged, sems):
    copies = [pltpu.make_async_copy(tiles_hbm, tiles, sems.at[0])]
    part = NT // 2
    for i in range(2):
        strip = pl.ds(i * part, part)
        copies.append(pltpu.make_async_copy(factors_hbm.at[:, strip], raw.at[:, strip], sems.at[1 + i]))
    for copy in copies:
        copy.start()
    copies[0].wait()
    lane = lax.broadcasted_iota(jnp.int32, (2, V), 1)
    tile_row = jnp.zeros((2, V), jnp.float32)
    for member in range(GROUP):
        for k in range(K):
            tile_row = jnp.where(lane == member * K + k, tiles[k, member].astype(jnp.float32), tile_row)
    for row in range(ROWS):
        staged[pl.ds(row * MSG1 + NT, 2), :] = tile_row
    for i in range(2):
        copies[1 + i].wait()
        for q in range(NQ):
            first = (q * NT + i * part) * ROWS
            wide[pl.ds(first, part * ROWS), :] = (
                raw[q, pl.ds(i * part, part)].astype(jnp.float32).reshape(part * ROWS, HALF)
            )
        for row in range(ROWS):
            for eight in range(part // 8):
                first = (i * part + eight * 8) * ROWS + row
                sides = [wide[pl.ds(q * NT * ROWS + first, 8, stride=ROWS), :] for q in range(NQ)]
                staged[pl.ds(row * MSG1 + i * part + eight * 8, 8), :] = jnp.concatenate(sides, axis=1)
    packed = staged[...].astype(jnp.bfloat16)
    for u in range(NU):
        out_ref[u] = packed


def scalar_of(row):
    return jnp.max(row).astype(jnp.int32)


def table_kernel(place_ref, held_ref, out_ref):
    start = pl.multiple_of(scalar_of(place_ref[0:1]) * (ROWS * MSG1), 16)
    for group in range(GROUP // 2):
        row = group * MSG1 + NT
        block = held_ref[pl.ds(pl.multiple_of(start + row // 16 * 16, 16), 16), :].astype(jnp.float32)
        named = block[row % 16 : row % 16 + 1].astype(jnp.int32)
        strip = ((named >> 2) & 1) * ROWS + (named >> 3) * NB + (named & (NB - 1))
        out_ref[pl.ds(group, 1), :] = 2 * named
        out_ref[pl.ds(GROUP // 2 + group, 1), :] = 2 * MSG1 * strip


def select_kernel(place_ref, table_ref, mine_ref, theirs_ref, out_ref, wide, staged, table, sem):
    copy = pltpu.make_async_copy(table_ref, table, sem)
    copy.start()
    core = scalar_of(place_ref[1:2])
    wide[pl.ds(core, HELD, stride=2), :] = mine_ref[...].astype(jnp.float32)
    wide[pl.ds(1 - core, HELD, stride=2), :] = theirs_ref[...].astype(jnp.float32)
    copy.wait()

    def one_group(group, carry):
        for parity in range(2):
            for y in range(NY):
                lanes = [(2 * y + parity) * K + k for k in range(K)]
                named = [table[group, lane] for lane in lanes]
                strips = [table[GROUP // 2 + group, lane] for lane in lanes]
                base = group * MSG2 + (y * ROWS + parity * (GROUP // 2)) * MSG2
                for l in range(K):
                    for k in range(K):
                        staged[pl.ds(base + (l * K + k) * 2, 2), :] = wide[
                            pl.ds(pl.multiple_of(strips[l] + named[k], 2), 2), :
                        ]
        return carry

    lax.fori_loop(0, GROUP // 2, one_group, 0)
    out_ref[...] = staged[...].astype(jnp.bfloat16)


ACROSS = (((1,), (1,)), ((), ()))


def ladder_kernel(place_ref, amps_ref, mirror_amps_ref, blocks_ref, sent_ref, domain, half, mirror_half, wide):
    wide[...] = blocks_ref[...].astype(jnp.float32)
    left = lax.broadcasted_iota(jnp.int32, (ROWS, V), 1) < HALF
    for y in range(NY):
        for l in range(K):
            for k in range(K):
                first = y * ROWS * MSG2 + (l * K + k) * 2
                sides = [wide[pl.ds(first + h, ROWS, stride=MSG2), :] for h in range(2)]
                rows = pl.ds(k * V + y * ROWS, ROWS)
                for q in range(NQ):
                    block = jnp.where(
                        left,
                        sides[0] if q == 0 else pltpu.roll(sides[0], HALF, 1),
                        sides[1] if q == 1 else pltpu.roll(sides[1], HALF, 1),
                    )
                    domain[rows, pl.ds(q * WIDTH + l * V, V)] = block.astype(jnp.bfloat16)
    own = amps_ref[scalar_of(place_ref[2:3])]
    both = jnp.concatenate([own, mirror_amps_ref[...]], axis=1)
    for q in range(NQ):
        columns = pl.ds(q * WIDTH, WIDTH)
        halves = jnp.dot(domain[:, columns], both, preferred_element_type=jnp.float32).astype(jnp.bfloat16)
        half[:, columns] = halves[:, :WIDTH]
        mirror_half[:, columns] = halves[:, WIDTH:]
    sent_ref[...] = (
        lax.dot_general(domain[...], half[...], ACROSS, preferred_element_type=jnp.float32)
        + lax.dot_general(mirror_half[...], domain[...], ACROSS, preferred_element_type=jnp.float32)
    ).astype(jnp.bfloat16)


def denominators_of(info_ref, tiles_ref, pair_energy_ref, energy_ref, slot):
    member = 2 * info_ref[3] + slot
    rows = [energy_ref[pl.ds(tiles_ref[k, member], 1), :] for k in range(K)]
    across = jnp.concatenate(rows, axis=1)
    bands = []
    for row in rows:
        down = jnp.transpose(jnp.broadcast_to(row, (V, V)))
        bands.append(jnp.concatenate([down] * K, axis=1) + across - pair_energy_ref[slot])
    return bands


def write_pair(slot, denominator_of, residual_of, amps_ref, residual_out, updated_out, residual_buf, updated_buf, sems):
    copies = []
    for step in range(K):
        band = pl.ds(step * V, V)
        residual = residual_of(band)
        residual_buf[band, :] = residual
        updated_buf[band, :] = (
            amps_ref[slot, band, :].astype(jnp.float32) - residual / denominator_of(step)
        ).astype(jnp.bfloat16)
        for buf, out, sem in (
            (residual_buf, residual_out, sems.at[0, step]),
            (updated_buf, updated_out, sems.at[1, step]),
        ):
            copy = pltpu.make_async_copy(buf.at[band, :], out.at[slot, band, :], sem)
            copy.start()
            copies.append(copy)
    for copy in copies:
        copy.wait()


def own_kernel(
    info_ref, tiles_ref, pair_energy_ref, energy_ref, amps_ref, domain, half, mirror_half,
    residual_out, updated_out, other_ref, residual_buf, updated_buf, sems,
):
    energies = (info_ref, tiles_ref, pair_energy_ref, energy_ref)
    slot = info_ref[2]
    for step, band in enumerate(denominators_of(*energies, 1 - slot)):
        other_ref[pl.ds(step * V, V), :] = band
    bands = denominators_of(*energies, slot)

    def residual_of(band):
        return lax.dot_general(
            half[band, :], domain[...], ACROSS, preferred_element_type=jnp.float32
        ) + lax.dot_general(domain[band, :], mirror_half[...], ACROSS, preferred_element_type=jnp.float32)

    write_pair(
        slot, lambda step: bands[step], residual_of, amps_ref,
        residual_out, updated_out, residual_buf, updated_buf, sems,
    )


def other_kernel(
    place_ref, amps_ref, received_ref, denominators_ref, residual_in, updated_in,
    residual_out, updated_out, residual_buf, updated_buf, sems,
):
    write_pair(
        1 - scalar_of(place_ref[2:3]),
        lambda step: denominators_ref[pl.ds(step * V, V), :],
        lambda band: received_ref[band, :].astype(jnp.float32),
        amps_ref, residual_out, updated_out, residual_buf, updated_buf, sems,
    )


def whole(space=VMEM):
    return pl.BlockSpec(memory_space=space)


def shards(amplitudes, factors, tiles, mirror, pair_energy, virt_energy):
    f32, bf16 = jnp.float32, jnp.bfloat16
    x = lax.axis_index("x")
    sel = jnp.where(x < NX // 2, 0, 1 - (mirror[0] & 1))
    info = jnp.stack([lax.axis_index(a) for a in ("u", "c")] + [sel, lax.axis_index("y")]).astype(jnp.int32)
    place = jnp.broadcast_to(info.astype(f32)[:, None], (4, V))
    tiles_t = tiles.T

    spread = pl.pallas_call(
        spread_kernel,
        out_shape=jax.ShapeDtypeStruct((NU, ROWS * MSG1, V), bf16),
        in_specs=[whole(pltpu.MemorySpace.HBM), whole(pltpu.MemorySpace.HBM)],
        out_specs=whole(),
        scratch_shapes=[
            pltpu.SMEM(tiles_t.shape, jnp.int32),
            pltpu.VMEM(factors.shape, bf16),
            pltpu.VMEM((NQ * NT * ROWS, HALF), f32),
            pltpu.VMEM((ROWS * MSG1, V), f32),
            pltpu.SemaphoreType.DMA((3,)),
        ],
        compiler_params=pltpu.CompilerParams(vmem_limit_bytes=60 * 1024 * 1024),
        name="spread",
    )(tiles_t, factors)
    held = lax.all_to_all(spread.reshape(SOURCES, MSG1 // 2, 2, V), ("u", "x", "b"), 0, 0, tiled=True)
    theirs = lax.ppermute(held, "c", [(1, 0), (0, 1)])
    going = lax.dynamic_index_in_dim(amplitudes, 1 - sel, 0, keepdims=False)
    opposite = [((i + NX // 2) % NX, i) for i in range(NX)]
    mirror_amps = lax.ppermute(going, "x", opposite)

    held = held.reshape(HELD, V)
    table = pl.pallas_call(
        table_kernel,
        out_shape=jax.ShapeDtypeStruct((GROUP, V), jnp.int32),
        in_specs=[whole(), whole()],
        out_specs=whole(),
        compiler_params=PARAMS,
        name="table",
    )(place, held)
    selected = pl.pallas_call(
        select_kernel,
        out_shape=jax.ShapeDtypeStruct((PLANE * MSG2, V), bf16),
        in_specs=[whole()] * 4,
        out_specs=whole(),
        scratch_shapes=[
            pltpu.VMEM((NC * HELD, V), f32),
            pltpu.VMEM((PLANE * MSG2, V), f32),
            pltpu.SMEM((GROUP, V), jnp.int32),
            pltpu.SemaphoreType.DMA,
        ],
        compiler_params=PARAMS,
        name="select",
    )(place, table, held, theirs.reshape(HELD, V))
    selected, mirror_amps = lax.optimization_barrier((selected, mirror_amps))
    blocks = lax.all_to_all(
        selected.reshape(PLANE, MSG2 // 2, 2, V), ("y", "x", "b"), 0, 0, tiled=True
    )

    wide_half = jax.ShapeDtypeStruct((WIDTH, NQ * WIDTH), bf16)
    sent, domain, half, mirror_half = pl.pallas_call(
        ladder_kernel,
        out_shape=(jax.ShapeDtypeStruct((WIDTH, WIDTH), bf16), wide_half, wide_half, wide_half),
        in_specs=[whole()] * 4,
        out_specs=(whole(),) * 4,
        scratch_shapes=[pltpu.VMEM((PLANE * MSG2, V), f32)],
        compiler_params=PARAMS,
        name="ladder",
    )(place, amplitudes, mirror_amps, blocks.reshape(PLANE * MSG2, V))
    received = lax.ppermute(sent, "x", opposite)

    energies = virt_energy.reshape(NT, V)
    outs = (
        jax.ShapeDtypeStruct(amplitudes.shape, f32),
        jax.ShapeDtypeStruct(amplitudes.shape, bf16),
    )
    buffers = [
        pltpu.VMEM((WIDTH, WIDTH), f32),
        pltpu.VMEM((WIDTH, WIDTH), bf16),
        pltpu.SemaphoreType.DMA((2, K)),
    ]
    residual, updated, denominators = pl.pallas_call(
        own_kernel,
        out_shape=outs + (jax.ShapeDtypeStruct((WIDTH, WIDTH), f32),),
        in_specs=[whole(SMEM)] * 3 + [whole()] * 5,
        out_specs=(whole(pl.ANY), whole(pl.ANY), whole()),
        scratch_shapes=buffers,
        cost_estimate=pl.CostEstimate(flops=8 * WIDTH**3, bytes_accessed=10 * WIDTH**2, transcendentals=0),
        compiler_params=PARAMS,
        name="own",
    )(info, tiles_t, pair_energy, energies, amplitudes, domain, half, mirror_half)
    residual, updated = pl.pallas_call(
        other_kernel,
        out_shape=outs,
        in_specs=[whole(), whole(), whole(), whole(), whole(pl.ANY), whole(pl.ANY)],
        out_specs=(whole(pl.ANY),) * 2,
        scratch_shapes=buffers,
        input_output_aliases={4: 0, 5: 1},
        cost_estimate=pl.CostEstimate(flops=4 * WIDTH**2, bytes_accessed=10 * WIDTH**2, transcendentals=0),
        compiler_params=PARAMS,
        name="other",
    )(place, amplitudes, received, denominators, residual, updated)
    return (residual, updated)


def solution(mesh):
    fine = Mesh(mesh.devices.reshape(NX, NU, NB, NC, NY), ("x", "u", "b", "c", "y"))
    pairs = ("x", "u", "b", "c")
    return jax.shard_map(
        shards,
        mesh=fine,
        in_specs=(
            P(pairs + ("y",), None, None),
            P(None, None, "y", pairs),
            P(pairs, None),
            P(pairs + ("y",)),
            P(pairs + ("y",)),
            P(),
        ),
        out_specs=(P(pairs + ("y",), None, None), P(pairs + ("y",), None, None)),
        check_vma=False,
    )
```

```python
import jax
import jax.numpy as jnp
from jax import lax
from jax.experimental import pallas as pl
from jax.experimental.pallas import tpu as pltpu
from jax.sharding import Mesh, PartitionSpec as P

V = 128
K = 3
NX, NU, NB, NC, NY = 4, 2, 4, 2, 8
NT = 32
NQ = 2
HALF = V // 2
GROUP = 16
WIDTH = K * V
ROWS = NX * NB
SOURCES = NU * ROWS
PLANE = ROWS * NY
MSG1 = NT + 2
HELD = SOURCES * MSG1
MSG2 = 2 * K * K
SMEM = pltpu.MemorySpace.SMEM
VMEM = pltpu.MemorySpace.VMEM
PARAMS = pltpu.CompilerParams(vmem_limit_bytes=24 * 1024 * 1024)


def spread_kernel(tiles_hbm, factors_hbm, out_ref, tiles, raw, wide, staged, sems):
    slots = [(row % NB) * NX + row // NB for row in range(ROWS)]
    copies = [pltpu.make_async_copy(tiles_hbm, tiles, sems.at[0])]
    part = NT // 2
    for i in range(2):
        strip = pl.ds(i * part, part)
        copies.append(pltpu.make_async_copy(factors_hbm.at[:, strip], raw.at[:, strip], sems.at[1 + i]))
    for copy in copies:
        copy.start()
    copies[0].wait()
    lane = lax.broadcasted_iota(jnp.int32, (2, V), 1)
    tile_row = jnp.zeros((2, V), jnp.float32)
    for member in range(GROUP):
        for k in range(K):
            tile_row = jnp.where(lane == member * K + k, tiles[k, member].astype(jnp.float32), tile_row)
    for row in range(ROWS):
        staged[pl.ds(slots[row] * MSG1 + NT, 2), :] = tile_row
    for i in range(2):
        copies[1 + i].wait()
        for q in range(NQ):
            first = (q * NT + i * part) * ROWS
            wide[pl.ds(first, part * ROWS), :] = (
                raw[q, pl.ds(i * part, part)].astype(jnp.float32).reshape(part * ROWS, HALF)
            )
        for row in range(ROWS):
            for eight in range(part // 8):
                first = (i * part + eight * 8) * ROWS + row
                sides = [wide[pl.ds(q * NT * ROWS + first, 8, stride=ROWS), :] for q in range(NQ)]
                staged[pl.ds(slots[row] * MSG1 + i * part + eight * 8, 8), :] = jnp.concatenate(sides, axis=1)
    packed = staged[...].astype(jnp.bfloat16)
    for u in range(NU):
        out_ref[u] = packed


def scalar_of(row):
    return jnp.max(row).astype(jnp.int32)


def table_kernel(place_ref, held_ref, out_ref):
    start = pl.multiple_of(scalar_of(place_ref[0:1]) * (ROWS * MSG1), 16)
    for group in range(GROUP // 2):
        row = (group % NB * NX + group // NB) * MSG1 + NT
        block = held_ref[pl.ds(pl.multiple_of(start + row // 16 * 16, 16), 16), :].astype(jnp.float32)
        named = block[row % 16 : row % 16 + 1].astype(jnp.int32)
        strip = ((named >> 2) & 1) * ROWS + (named & (NB - 1)) * NX + (named >> 3)
        out_ref[pl.ds(group, 1), :] = 2 * named
        out_ref[pl.ds(GROUP // 2 + group, 1), :] = 2 * MSG1 * strip


def select_kernel(place_ref, table_ref, mine_ref, theirs_ref, out_ref, wide, staged, table, sem):
    copy = pltpu.make_async_copy(table_ref, table, sem)
    copy.start()
    core = scalar_of(place_ref[1:2])
    wide[pl.ds(core, HELD, stride=2), :] = mine_ref[...].astype(jnp.float32)
    wide[pl.ds(1 - core, HELD, stride=2), :] = theirs_ref[...].astype(jnp.float32)
    copy.wait()

    def one_group(group, carry):
        first = (group // NB * (NY * NB) + group % NB) * MSG2
        for parity in range(2):
            for y in range(NY):
                lanes = [(2 * y + parity) * K + k for k in range(K)]
                named = [table[group, lane] for lane in lanes]
                strips = [table[GROUP // 2 + group, lane] for lane in lanes]
                base = first + (parity * (NX // 2) * NY + y) * NB * MSG2
                for l in range(K):
                    for k in range(K):
                        staged[pl.ds(base + (l * K + k) * 2, 2), :] = wide[
                            pl.ds(pl.multiple_of(strips[l] + named[k], 2), 2), :
                        ]
        return carry

    lax.fori_loop(0, GROUP // 2, one_group, 0)
    out_ref[...] = staged[...].astype(jnp.bfloat16)


ACROSS = (((1,), (1,)), ((), ()))


def ladder_kernel(place_ref, amps_ref, mirror_amps_ref, blocks_ref, sent_ref, domain, half, mirror_half, wide):
    run = NB * MSG2
    for x in range(NX):
        for y in range(0, NY, 2):
            chunk = blocks_ref[pl.ds((x * NY + y) * run, 2 * run), :].astype(jnp.float32)
            wide[pl.ds((y * NX + x) * run, run), :] = chunk[:run]
            wide[pl.ds(((y + 1) * NX + x) * run, run), :] = chunk[run:]
    left = lax.broadcasted_iota(jnp.int32, (ROWS, V), 1) < HALF
    for y in range(NY):
        for l in range(K):
            for k in range(K):
                first = y * ROWS * MSG2 + (l * K + k) * 2
                sides = [wide[pl.ds(first + h, ROWS, stride=MSG2), :] for h in range(2)]
                rows = pl.ds(k * V + y * ROWS, ROWS)
                for q in range(NQ):
                    block = jnp.where(
                        left,
                        sides[0] if q == 0 else pltpu.roll(sides[0], HALF, 1),
                        sides[1] if q == 1 else pltpu.roll(sides[1], HALF, 1),
                    )
                    domain[rows, pl.ds(q * WIDTH + l * V, V)] = block.astype(jnp.bfloat16)
    own = amps_ref[scalar_of(place_ref[2:3])]
    both = jnp.concatenate([own, mirror_amps_ref[...]], axis=1)
    for q in range(NQ):
        columns = pl.ds(q * WIDTH, WIDTH)
        halves = jnp.dot(domain[:, columns], both, preferred_element_type=jnp.float32).astype(jnp.bfloat16)
        half[:, columns] = halves[:, :WIDTH]
        mirror_half[:, columns] = halves[:, WIDTH:]
    sent_ref[...] = (
        lax.dot_general(domain[...], half[...], ACROSS, preferred_element_type=jnp.float32)
        + lax.dot_general(mirror_half[...], domain[...], ACROSS, preferred_element_type=jnp.float32)
    ).astype(jnp.bfloat16)


def denominators_of(info_ref, tiles_ref, pair_energy_ref, energy_ref, slot):
    member = 2 * info_ref[3] + slot
    rows = [energy_ref[pl.ds(tiles_ref[k, member], 1), :] for k in range(K)]
    across = jnp.concatenate(rows, axis=1)
    bands = []
    for row in rows:
        down = jnp.transpose(jnp.broadcast_to(row, (V, V)))
        bands.append(jnp.concatenate([down] * K, axis=1) + across - pair_energy_ref[slot])
    return bands


def write_pair(slot, denominator_of, residual_of, amps_ref, residual_out, updated_out, residual_buf, updated_buf, sems):
    copies = []
    for step in range(K):
        band = pl.ds(step * V, V)
        residual = residual_of(band)
        residual_buf[band, :] = residual
        updated_buf[band, :] = (
            amps_ref[slot, band, :].astype(jnp.float32) - residual / denominator_of(step)
        ).astype(jnp.bfloat16)
        for buf, out, sem in (
            (residual_buf, residual_out, sems.at[0, step]),
            (updated_buf, updated_out, sems.at[1, step]),
        ):
            copy = pltpu.make_async_copy(buf.at[band, :], out.at[slot, band, :], sem)
            copy.start()
            copies.append(copy)
    for copy in copies:
        copy.wait()


def own_kernel(
    info_ref, tiles_ref, pair_energy_ref, energy_ref, amps_ref, domain, half, mirror_half,
    residual_out, updated_out, other_ref, residual_buf, updated_buf, sems,
):
    energies = (info_ref, tiles_ref, pair_energy_ref, energy_ref)
    slot = info_ref[2]
    for step, band in enumerate(denominators_of(*energies, 1 - slot)):
        other_ref[pl.ds(step * V, V), :] = band
    bands = denominators_of(*energies, slot)

    def residual_of(band):
        return lax.dot_general(
            half[band, :], domain[...], ACROSS, preferred_element_type=jnp.float32
        ) + lax.dot_general(domain[band, :], mirror_half[...], ACROSS, preferred_element_type=jnp.float32)

    write_pair(
        slot, lambda step: bands[step], residual_of, amps_ref,
        residual_out, updated_out, residual_buf, updated_buf, sems,
    )


def other_kernel(
    place_ref, amps_ref, received_ref, denominators_ref, residual_in, updated_in,
    residual_out, updated_out, residual_buf, updated_buf, sems,
):
    write_pair(
        1 - scalar_of(place_ref[2:3]),
        lambda step: denominators_ref[pl.ds(step * V, V), :],
        lambda band: received_ref[band, :].astype(jnp.float32),
        amps_ref, residual_out, updated_out, residual_buf, updated_buf, sems,
    )


def whole(space=VMEM):
    return pl.BlockSpec(memory_space=space)


def shards(amplitudes, factors, tiles, mirror, pair_energy, virt_energy):
    f32, bf16 = jnp.float32, jnp.bfloat16
    x = lax.axis_index("x")
    sel = jnp.where(x < NX // 2, 0, 1 - (mirror[0] & 1))
    info = jnp.stack([lax.axis_index(a) for a in ("u", "c")] + [sel, lax.axis_index("y")]).astype(jnp.int32)
    place = jnp.broadcast_to(info.astype(f32)[:, None], (4, V))
    tiles_t = tiles.T

    spread = pl.pallas_call(
        spread_kernel,
        out_shape=jax.ShapeDtypeStruct((NU, ROWS * MSG1, V), bf16),
        in_specs=[whole(pltpu.MemorySpace.HBM), whole(pltpu.MemorySpace.HBM)],
        out_specs=whole(),
        scratch_shapes=[
            pltpu.SMEM(tiles_t.shape, jnp.int32),
            pltpu.VMEM(factors.shape, bf16),
            pltpu.VMEM((NQ * NT * ROWS, HALF), f32),
            pltpu.VMEM((ROWS * MSG1, V), f32),
            pltpu.SemaphoreType.DMA((3,)),
        ],
        compiler_params=pltpu.CompilerParams(vmem_limit_bytes=60 * 1024 * 1024),
        name="spread",
    )(tiles_t, factors)
    held = lax.all_to_all(spread.reshape(SOURCES, MSG1 // 2, 2, V), ("u", "b", "x"), 0, 0, tiled=True)
    theirs = lax.ppermute(held, "c", [(1, 0), (0, 1)])
    going = lax.dynamic_index_in_dim(amplitudes, 1 - sel, 0, keepdims=False)
    opposite = [((i + NX // 2) % NX, i) for i in range(NX)]
    mirror_amps = lax.ppermute(going, "x", opposite)

    held = held.reshape(HELD, V)
    table = pl.pallas_call(
        table_kernel,
        out_shape=jax.ShapeDtypeStruct((GROUP, V), jnp.int32),
        in_specs=[whole(), whole()],
        out_specs=whole(),
        compiler_params=PARAMS,
        name="table",
    )(place, held)
    selected = pl.pallas_call(
        select_kernel,
        out_shape=jax.ShapeDtypeStruct((PLANE * MSG2, V), bf16),
        in_specs=[whole()] * 4,
        out_specs=whole(),
        scratch_shapes=[
            pltpu.VMEM((NC * HELD, V), f32),
            pltpu.VMEM((PLANE * MSG2, V), f32),
            pltpu.SMEM((GROUP, V), jnp.int32),
            pltpu.SemaphoreType.DMA,
        ],
        compiler_params=PARAMS,
        name="select",
    )(place, table, held, theirs.reshape(HELD, V))
    selected, mirror_amps = lax.optimization_barrier((selected, mirror_amps))
    blocks = lax.all_to_all(
        selected.reshape(PLANE, MSG2 // 2, 2, V), ("x", "y", "b"), 0, 0, tiled=True
    )

    wide_half = jax.ShapeDtypeStruct((WIDTH, NQ * WIDTH), bf16)
    sent, domain, half, mirror_half = pl.pallas_call(
        ladder_kernel,
        out_shape=(jax.ShapeDtypeStruct((WIDTH, WIDTH), bf16), wide_half, wide_half, wide_half),
        in_specs=[whole()] * 4,
        out_specs=(whole(),) * 4,
        scratch_shapes=[pltpu.VMEM((PLANE * MSG2, V), f32)],
        compiler_params=PARAMS,
        name="ladder",
    )(place, amplitudes, mirror_amps, blocks.reshape(PLANE * MSG2, V))
    received = lax.ppermute(sent, "x", opposite)

    energies = virt_energy.reshape(NT, V)
    outs = (
        jax.ShapeDtypeStruct(amplitudes.shape, f32),
        jax.ShapeDtypeStruct(amplitudes.shape, bf16),
    )
    buffers = [
        pltpu.VMEM((WIDTH, WIDTH), f32),
        pltpu.VMEM((WIDTH, WIDTH), bf16),
        pltpu.SemaphoreType.DMA((2, K)),
    ]
    residual, updated, denominators = pl.pallas_call(
        own_kernel,
        out_shape=outs + (jax.ShapeDtypeStruct((WIDTH, WIDTH), f32),),
        in_specs=[whole(SMEM)] * 3 + [whole()] * 5,
        out_specs=(whole(pl.ANY), whole(pl.ANY), whole()),
        scratch_shapes=buffers,
        cost_estimate=pl.CostEstimate(flops=8 * WIDTH**3, bytes_accessed=10 * WIDTH**2, transcendentals=0),
        compiler_params=PARAMS,
        name="own",
    )(info, tiles_t, pair_energy, energies, amplitudes, domain, half, mirror_half)
    residual, updated = pl.pallas_call(
        other_kernel,
        out_shape=outs,
        in_specs=[whole(), whole(), whole(), whole(), whole(pl.ANY), whole(pl.ANY)],
        out_specs=(whole(pl.ANY),) * 2,
        scratch_shapes=buffers,
        input_output_aliases={4: 0, 5: 1},
        cost_estimate=pl.CostEstimate(flops=4 * WIDTH**2, bytes_accessed=10 * WIDTH**2, transcendentals=0),
        compiler_params=PARAMS,
        name="other",
    )(place, amplitudes, received, denominators, residual, updated)
    return (residual, updated)


def solution(mesh):
    fine = Mesh(mesh.devices.reshape(NX, NU, NB, NC, NY), ("x", "u", "b", "c", "y"))
    pairs = ("x", "u", "b", "c")
    return jax.shard_map(
        shards,
        mesh=fine,
        in_specs=(
            P(pairs + ("y",), None, None),
            P(None, None, "y", pairs),
            P(pairs, None),
            P(pairs + ("y",)),
            P(pairs + ("y",)),
            P(),
        ),
        out_specs=(P(pairs + ("y",), None, None), P(pairs + ("y",), None, None)),
        check_vma=False,
    )
```

```python
import jax
import jax.numpy as jnp
from jax import lax
from jax.experimental import pallas as pl
from jax.experimental.pallas import tpu as pltpu
from jax.sharding import Mesh, PartitionSpec as P

V = 128
K = 3
NX, NU, NB, NC, NY = 4, 2, 4, 2, 8
NT = 32
NQ = 2
HALF = V // 2
GROUP = 16
WIDTH = K * V
ROWS = NX * NB
SOURCES = NU * ROWS
PLANE = ROWS * NY
MSG1 = NT + 2
HELD = SOURCES * MSG1
MSG2 = 2 * K * K
SMEM = pltpu.MemorySpace.SMEM
VMEM = pltpu.MemorySpace.VMEM
PARAMS = pltpu.CompilerParams(vmem_limit_bytes=24 * 1024 * 1024)


def spread_kernel(tiles_hbm, factors_hbm, out_ref, tiles, raw, wide, staged, sems):
    slots = [(row % NB) * NX + row // NB for row in range(ROWS)]
    copies = [pltpu.make_async_copy(tiles_hbm, tiles, sems.at[0])]
    part = NT // 2
    for i in range(2):
        strip = pl.ds(i * part, part)
        copies.append(pltpu.make_async_copy(factors_hbm.at[:, strip], raw.at[:, strip], sems.at[1 + i]))
    for copy in copies:
        copy.start()
    copies[0].wait()
    lane = lax.broadcasted_iota(jnp.int32, (2, V), 1)
    tile_row = jnp.zeros((2, V), jnp.float32)
    for member in range(GROUP):
        for k in range(K):
            tile_row = jnp.where(lane == member * K + k, tiles[k, member].astype(jnp.float32), tile_row)
    for row in range(ROWS):
        staged[pl.ds(slots[row] * MSG1 + NT, 2), :] = tile_row
    for i in range(2):
        copies[1 + i].wait()
        for q in range(NQ):
            first = (q * NT + i * part) * ROWS
            wide[pl.ds(first, part * ROWS), :] = (
                raw[q, pl.ds(i * part, part)].astype(jnp.float32).reshape(part * ROWS, HALF)
            )
        for row in range(ROWS):
            for eight in range(part // 8):
                first = (i * part + eight * 8) * ROWS + row
                sides = [wide[pl.ds(q * NT * ROWS + first, 8, stride=ROWS), :] for q in range(NQ)]
                staged[pl.ds(slots[row] * MSG1 + i * part + eight * 8, 8), :] = jnp.concatenate(sides, axis=1)
    packed = staged[...].astype(jnp.bfloat16)
    for u in range(NU):
        out_ref[u] = packed


def scalar_of(row):
    return jnp.max(row).astype(jnp.int32)


def table_kernel(place_ref, held_ref, out_ref):
    start = pl.multiple_of(scalar_of(place_ref[0:1]) * (ROWS * MSG1), 16)
    for group in range(GROUP // 2):
        row = (group % NB * NX + group // NB) * MSG1 + NT
        block = held_ref[pl.ds(pl.multiple_of(start + row // 16 * 16, 16), 16), :].astype(jnp.float32)
        named = block[row % 16 : row % 16 + 1].astype(jnp.int32)
        strip = ((named >> 2) & 1) * ROWS + (named & (NB - 1)) * NX + (named >> 3)
        out_ref[pl.ds(group, 1), :] = 2 * named
        out_ref[pl.ds(GROUP // 2 + group, 1), :] = 2 * MSG1 * strip


def select_kernel(place_ref, table_ref, mine_ref, theirs_ref, out_ref, wide, staged, table, sem):
    copy = pltpu.make_async_copy(table_ref, table, sem)
    copy.start()
    core = scalar_of(place_ref[1:2])
    wide[pl.ds(core, HELD, stride=2), :] = mine_ref[...].astype(jnp.float32)
    wide[pl.ds(1 - core, HELD, stride=2), :] = theirs_ref[...].astype(jnp.float32)
    copy.wait()

    def one_group(group, carry):
        first = (group // NB * (NX // 2 * NY * NB) + group % NB) * MSG2
        for parity in range(2):
            for y in range(NY):
                lanes = [(2 * y + parity) * K + k for k in range(K)]
                named = [table[group, lane] for lane in lanes]
                strips = [table[GROUP // 2 + group, lane] for lane in lanes]
                base = first + (parity * NY + y) * NB * MSG2
                for l in range(K):
                    for k in range(K):
                        staged[pl.ds(base + (l * K + k) * 2, 2), :] = wide[
                            pl.ds(pl.multiple_of(strips[l] + named[k], 2), 2), :
                        ]
        return carry

    lax.fori_loop(0, GROUP // 2, one_group, 0)
    out_ref[...] = staged[...].astype(jnp.bfloat16)


ACROSS = (((1,), (1,)), ((), ()))


def ladder_kernel(place_ref, amps_ref, mirror_amps_ref, blocks_ref, sent_ref, domain, half, mirror_half, wide):
    run = NB * MSG2
    for x in range(NX):
        for y in range(0, NY, 2):
            place = x % 2 * (NX // 2) + x // 2
            chunk = blocks_ref[pl.ds((place * NY + y) * run, 2 * run), :].astype(jnp.float32)
            wide[pl.ds((y * NX + x) * run, run), :] = chunk[:run]
            wide[pl.ds(((y + 1) * NX + x) * run, run), :] = chunk[run:]
    left = lax.broadcasted_iota(jnp.int32, (ROWS, V), 1) < HALF
    for y in range(NY):
        for l in range(K):
            for k in range(K):
                first = y * ROWS * MSG2 + (l * K + k) * 2
                sides = [wide[pl.ds(first + h, ROWS, stride=MSG2), :] for h in range(2)]
                rows = pl.ds(k * V + y * ROWS, ROWS)
                for q in range(NQ):
                    block = jnp.where(
                        left,
                        sides[0] if q == 0 else pltpu.roll(sides[0], HALF, 1),
                        sides[1] if q == 1 else pltpu.roll(sides[1], HALF, 1),
                    )
                    domain[rows, pl.ds(q * WIDTH + l * V, V)] = block.astype(jnp.bfloat16)
    own = amps_ref[scalar_of(place_ref[2:3])]
    both = jnp.concatenate([own, mirror_amps_ref[...]], axis=1)
    for q in range(NQ):
        columns = pl.ds(q * WIDTH, WIDTH)
        halves = jnp.dot(domain[:, columns], both, preferred_element_type=jnp.float32).astype(jnp.bfloat16)
        half[:, columns] = halves[:, :WIDTH]
        mirror_half[:, columns] = halves[:, WIDTH:]
    sent_ref[...] = (
        lax.dot_general(domain[...], half[...], ACROSS, preferred_element_type=jnp.float32)
        + lax.dot_general(mirror_half[...], domain[...], ACROSS, preferred_element_type=jnp.float32)
    ).astype(jnp.bfloat16)


def denominators_of(info_ref, tiles_ref, pair_energy_ref, energy_ref, slot):
    member = 2 * info_ref[3] + slot
    rows = [energy_ref[pl.ds(tiles_ref[k, member], 1), :] for k in range(K)]
    across = jnp.concatenate(rows, axis=1)
    bands = []
    for row in rows:
        down = jnp.transpose(jnp.broadcast_to(row, (V, V)))
        bands.append(jnp.concatenate([down] * K, axis=1) + across - pair_energy_ref[slot])
    return bands


def write_pair(slot, denominator_of, residual_of, amps_ref, residual_out, updated_out, residual_buf, updated_buf, sems):
    copies = []
    for step in range(K):
        band = pl.ds(step * V, V)
        residual = residual_of(band)
        residual_buf[band, :] = residual
        updated_buf[band, :] = (
            amps_ref[slot, band, :].astype(jnp.float32) - residual / denominator_of(step)
        ).astype(jnp.bfloat16)
        for buf, out, sem in (
            (residual_buf, residual_out, sems.at[0, step]),
            (updated_buf, updated_out, sems.at[1, step]),
        ):
            copy = pltpu.make_async_copy(buf.at[band, :], out.at[slot, band, :], sem)
            copy.start()
            copies.append(copy)
    for copy in copies:
        copy.wait()


def own_kernel(
    info_ref, tiles_ref, pair_energy_ref, energy_ref, amps_ref, domain, half, mirror_half,
    residual_out, updated_out, other_ref, residual_buf, updated_buf, sems,
):
    energies = (info_ref, tiles_ref, pair_energy_ref, energy_ref)
    slot = info_ref[2]
    for step, band in enumerate(denominators_of(*energies, 1 - slot)):
        other_ref[pl.ds(step * V, V), :] = band
    bands = denominators_of(*energies, slot)

    def residual_of(band):
        return lax.dot_general(
            half[band, :], domain[...], ACROSS, preferred_element_type=jnp.float32
        ) + lax.dot_general(domain[band, :], mirror_half[...], ACROSS, preferred_element_type=jnp.float32)

    write_pair(
        slot, lambda step: bands[step], residual_of, amps_ref,
        residual_out, updated_out, residual_buf, updated_buf, sems,
    )


def other_kernel(
    place_ref, amps_ref, received_ref, denominators_ref, residual_in, updated_in,
    residual_out, updated_out, residual_buf, updated_buf, sems,
):
    write_pair(
        1 - scalar_of(place_ref[2:3]),
        lambda step: denominators_ref[pl.ds(step * V, V), :],
        lambda band: received_ref[band, :].astype(jnp.float32),
        amps_ref, residual_out, updated_out, residual_buf, updated_buf, sems,
    )


def whole(space=VMEM):
    return pl.BlockSpec(memory_space=space)


def shards(amplitudes, factors, tiles, mirror, pair_energy, virt_energy):
    f32, bf16 = jnp.float32, jnp.bfloat16
    sel = jnp.where(lax.axis_index("xa") == 0, 0, 1 - (mirror[0] & 1))
    info = jnp.stack([lax.axis_index(a) for a in ("u", "c")] + [sel, lax.axis_index("y")]).astype(jnp.int32)
    place = jnp.broadcast_to(info.astype(f32)[:, None], (4, V))
    tiles_t = tiles.T

    spread = pl.pallas_call(
        spread_kernel,
        out_shape=jax.ShapeDtypeStruct((NU, ROWS * MSG1, V), bf16),
        in_specs=[whole(pltpu.MemorySpace.HBM), whole(pltpu.MemorySpace.HBM)],
        out_specs=whole(),
        scratch_shapes=[
            pltpu.SMEM(tiles_t.shape, jnp.int32),
            pltpu.VMEM(factors.shape, bf16),
            pltpu.VMEM((NQ * NT * ROWS, HALF), f32),
            pltpu.VMEM((ROWS * MSG1, V), f32),
            pltpu.SemaphoreType.DMA((3,)),
        ],
        compiler_params=pltpu.CompilerParams(vmem_limit_bytes=60 * 1024 * 1024),
        name="spread",
    )(tiles_t, factors)
    held = lax.all_to_all(spread.reshape(SOURCES, MSG1 // 2, 2, V), ("u", "b", "xa", "xb"), 0, 0, tiled=True)
    theirs = lax.ppermute(held, "c", [(1, 0), (0, 1)])
    going = lax.dynamic_index_in_dim(amplitudes, 1 - sel, 0, keepdims=False)
    opposite = [(1, 0), (0, 1)]
    mirror_amps = lax.ppermute(going, "xa", opposite)

    held = held.reshape(HELD, V)
    table = pl.pallas_call(
        table_kernel,
        out_shape=jax.ShapeDtypeStruct((GROUP, V), jnp.int32),
        in_specs=[whole(), whole()],
        out_specs=whole(),
        compiler_params=PARAMS,
        name="table",
    )(place, held)
    selected = pl.pallas_call(
        select_kernel,
        out_shape=jax.ShapeDtypeStruct((PLANE * MSG2, V), bf16),
        in_specs=[whole()] * 4,
        out_specs=whole(),
        scratch_shapes=[
            pltpu.VMEM((NC * HELD, V), f32),
            pltpu.VMEM((PLANE * MSG2, V), f32),
            pltpu.SMEM((GROUP, V), jnp.int32),
            pltpu.SemaphoreType.DMA,
        ],
        compiler_params=PARAMS,
        name="select",
    )(place, table, held, theirs.reshape(HELD, V))
    selected, mirror_amps = lax.optimization_barrier((selected, mirror_amps))
    blocks = lax.all_to_all(
        selected.reshape(PLANE, MSG2 // 2, 2, V), ("xb", "xa", "y", "b"), 0, 0, tiled=True
    )

    wide_half = jax.ShapeDtypeStruct((WIDTH, NQ * WIDTH), bf16)
    sent, domain, half, mirror_half = pl.pallas_call(
        ladder_kernel,
        out_shape=(jax.ShapeDtypeStruct((WIDTH, WIDTH), bf16), wide_half, wide_half, wide_half),
        in_specs=[whole()] * 4,
        out_specs=(whole(),) * 4,
        scratch_shapes=[pltpu.VMEM((PLANE * MSG2, V), f32)],
        compiler_params=PARAMS,
        name="ladder",
    )(place, amplitudes, mirror_amps, blocks.reshape(PLANE * MSG2, V))
    received = lax.ppermute(sent, "xa", opposite)

    energies = virt_energy.reshape(NT, V)
    outs = (
        jax.ShapeDtypeStruct(amplitudes.shape, f32),
        jax.ShapeDtypeStruct(amplitudes.shape, bf16),
    )
    buffers = [
        pltpu.VMEM((WIDTH, WIDTH), f32),
        pltpu.VMEM((WIDTH, WIDTH), bf16),
        pltpu.SemaphoreType.DMA((2, K)),
    ]
    residual, updated, denominators = pl.pallas_call(
        own_kernel,
        out_shape=outs + (jax.ShapeDtypeStruct((WIDTH, WIDTH), f32),),
        in_specs=[whole(SMEM)] * 3 + [whole()] * 5,
        out_specs=(whole(pl.ANY), whole(pl.ANY), whole()),
        scratch_shapes=buffers,
        cost_estimate=pl.CostEstimate(flops=8 * WIDTH**3, bytes_accessed=10 * WIDTH**2, transcendentals=0),
        compiler_params=PARAMS,
        name="own",
    )(info, tiles_t, pair_energy, energies, amplitudes, domain, half, mirror_half)
    residual, updated = pl.pallas_call(
        other_kernel,
        out_shape=outs,
        in_specs=[whole(), whole(), whole(), whole(), whole(pl.ANY), whole(pl.ANY)],
        out_specs=(whole(pl.ANY),) * 2,
        scratch_shapes=buffers,
        input_output_aliases={4: 0, 5: 1},
        cost_estimate=pl.CostEstimate(flops=4 * WIDTH**2, bytes_accessed=10 * WIDTH**2, transcendentals=0),
        compiler_params=PARAMS,
        name="other",
    )(place, amplitudes, received, denominators, residual, updated)
    return (residual, updated)


def solution(mesh):
    fine = Mesh(mesh.devices.reshape(2, NX // 2, NU, NB, NC, NY), ("xa", "xb", "u", "b", "c", "y"))
    pairs = ("xa", "xb", "u", "b", "c")
    return jax.shard_map(
        shards,
        mesh=fine,
        in_specs=(
            P(pairs + ("y",), None, None),
            P(None, None, "y", pairs),
            P(pairs, None),
            P(pairs + ("y",)),
            P(pairs + ("y",)),
            P(),
        ),
        out_specs=(P(pairs + ("y",), None, None), P(pairs + ("y",), None, None)),
        check_vma=False,
    )
```

```python
import jax
import jax.numpy as jnp
from jax import lax
from jax.experimental import pallas as pl
from jax.experimental.pallas import tpu as pltpu
from jax.sharding import Mesh, PartitionSpec as P

V = 128
K = 3
NX, NU, NB, NC, NY = 4, 2, 4, 2, 8
NT = 32
NQ = 2
HALF = V // 2
GROUP = 16
WIDTH = K * V
ROWS = NX * NB
SOURCES = NU * ROWS
PLANE = ROWS * NY
MSG1 = NT + 2
HELD = SOURCES * MSG1
MSG2 = 2 * K * K
SMEM = pltpu.MemorySpace.SMEM
VMEM = pltpu.MemorySpace.VMEM
PARAMS = pltpu.CompilerParams(vmem_limit_bytes=24 * 1024 * 1024)


def spread_kernel(tiles_hbm, factors_hbm, out_ref, tiles, raw, wide, staged, sems):
    slots = [(row % NB) * NX + row // NB for row in range(ROWS)]
    copies = [pltpu.make_async_copy(tiles_hbm, tiles, sems.at[0])]
    part = NT // 2
    for i in range(2):
        strip = pl.ds(i * part, part)
        copies.append(pltpu.make_async_copy(factors_hbm.at[:, strip], raw.at[:, strip], sems.at[1 + i]))
    for copy in copies:
        copy.start()
    copies[0].wait()
    lane = lax.broadcasted_iota(jnp.int32, (2, V), 1)
    tile_row = jnp.zeros((2, V), jnp.float32)
    for member in range(GROUP):
        for k in range(K):
            tile_row = jnp.where(lane == member * K + k, tiles[k, member].astype(jnp.float32), tile_row)
    for row in range(ROWS):
        staged[pl.ds(slots[row] * MSG1 + NT, 2), :] = tile_row
    for i in range(2):
        copies[1 + i].wait()
        for q in range(NQ):
            first = (q * NT + i * part) * ROWS
            wide[pl.ds(first, part * ROWS), :] = (
                raw[q, pl.ds(i * part, part)].astype(jnp.float32).reshape(part * ROWS, HALF)
            )
        for row in range(ROWS):
            for eight in range(part // 8):
                first = (i * part + eight * 8) * ROWS + row
                sides = [wide[pl.ds(q * NT * ROWS + first, 8, stride=ROWS), :] for q in range(NQ)]
                staged[pl.ds(slots[row] * MSG1 + i * part + eight * 8, 8), :] = jnp.concatenate(sides, axis=1)
    packed = staged[...].astype(jnp.bfloat16)
    for u in range(NU):
        out_ref[u] = packed


def scalar_of(row):
    return jnp.max(row).astype(jnp.int32)


def table_kernel(place_ref, held_ref, out_ref):
    start = pl.multiple_of(scalar_of(place_ref[0:1]) * (ROWS * MSG1), 16)
    for group in range(GROUP // 2):
        row = (group % NB * NX + group // NB) * MSG1 + NT
        block = held_ref[pl.ds(pl.multiple_of(start + row // 16 * 16, 16), 16), :].astype(jnp.float32)
        named = block[row % 16 : row % 16 + 1].astype(jnp.int32)
        strip = ((named >> 2) & 1) * ROWS + (named & (NB - 1)) * NX + (named >> 3)
        out_ref[pl.ds(group, 1), :] = 2 * named
        out_ref[pl.ds(GROUP // 2 + group, 1), :] = 2 * MSG1 * strip


def select_kernel(place_ref, table_ref, mine_ref, theirs_ref, out_ref, wide, staged, table, sem):
    copy = pltpu.make_async_copy(table_ref, table, sem)
    copy.start()
    core = scalar_of(place_ref[1:2])
    wide[pl.ds(core, HELD, stride=2), :] = mine_ref[...].astype(jnp.float32)
    wide[pl.ds(1 - core, HELD, stride=2), :] = theirs_ref[...].astype(jnp.float32)
    copy.wait()

    def one_group(group, carry):
        first = (group // NB * (NX // 2 * NY * NB) + group % NB) * MSG2
        for parity in range(2):
            for y in range(NY):
                lanes = [(2 * y + parity) * K + k for k in range(K)]
                named = [table[group, lane] for lane in lanes]
                strips = [table[GROUP // 2 + group, lane] for lane in lanes]
                base = first + (parity * NY + y) * NB * MSG2
                for l in range(K):
                    for k in range(K):
                        staged[pl.ds(base + (l * K + k) * 2, 2), :] = wide[
                            pl.ds(pl.multiple_of(strips[l] + named[k], 2), 2), :
                        ]
        return carry

    lax.fori_loop(0, GROUP // 2, one_group, 0)
    out_ref[...] = staged[...].astype(jnp.bfloat16)


ACROSS = (((1,), (1,)), ((), ()))


def ladder_kernel(place_ref, amps_ref, mirror_amps_ref, blocks_ref, sent_ref, domain, half, mirror_half, wide):
    run = NB * MSG2
    for x in range(NX):
        for y in range(0, NY, 2):
            place = x % 2 * (NX // 2) + x // 2
            chunk = blocks_ref[pl.ds((place * NY + y) * run, 2 * run), :].astype(jnp.float32)
            wide[pl.ds((y * NX + x) * run, run), :] = chunk[:run]
            wide[pl.ds(((y + 1) * NX + x) * run, run), :] = chunk[run:]
    left = lax.broadcasted_iota(jnp.int32, (ROWS, V), 1) < HALF
    for y in range(NY):
        for l in range(K):
            for k in range(K):
                first = y * ROWS * MSG2 + (l * K + k) * 2
                sides = [wide[pl.ds(first + h, ROWS, stride=MSG2), :] for h in range(2)]
                rows = pl.ds(k * V + y * ROWS, ROWS)
                for q in range(NQ):
                    block = jnp.where(
                        left,
                        sides[0] if q == 0 else pltpu.roll(sides[0], HALF, 1),
                        sides[1] if q == 1 else pltpu.roll(sides[1], HALF, 1),
                    )
                    domain[rows, pl.ds(q * WIDTH + l * V, V)] = block.astype(jnp.bfloat16)
    own = amps_ref[scalar_of(place_ref[2:3])]
    both = jnp.concatenate([own, mirror_amps_ref[...]], axis=1)
    for q in range(NQ):
        columns = pl.ds(q * WIDTH, WIDTH)
        halves = jnp.dot(domain[:, columns], both, preferred_element_type=jnp.float32).astype(jnp.bfloat16)
        half[:, columns] = halves[:, :WIDTH]
        mirror_half[:, columns] = halves[:, WIDTH:]
    sent_ref[...] = (
        lax.dot_general(domain[...], half[...], ACROSS, preferred_element_type=jnp.float32)
        + lax.dot_general(mirror_half[...], domain[...], ACROSS, preferred_element_type=jnp.float32)
    ).astype(jnp.bfloat16)


def denominators_of(info_ref, tiles_ref, pair_energy_ref, energy_ref, slot):
    member = 2 * info_ref[3] + slot
    rows = [energy_ref[pl.ds(tiles_ref[k, member], 1), :] for k in range(K)]
    across = jnp.concatenate(rows, axis=1)
    bands = []
    for row in rows:
        down = jnp.transpose(jnp.broadcast_to(row, (V, V)))
        bands.append(jnp.concatenate([down] * K, axis=1) + across - pair_energy_ref[slot])
    return bands


def write_pair(slot, denominator_of, residual_of, amps_ref, residual_out, updated_out, residual_buf, updated_buf, sems):
    copies = []
    for step in range(K):
        band = pl.ds(step * V, V)
        residual = residual_of(band)
        residual_buf[band, :] = residual
        updated_buf[band, :] = (
            amps_ref[slot, band, :].astype(jnp.float32) - residual / denominator_of(step)
        ).astype(jnp.bfloat16)
        for buf, out, sem in (
            (residual_buf, residual_out, sems.at[0, step]),
            (updated_buf, updated_out, sems.at[1, step]),
        ):
            copy = pltpu.make_async_copy(buf.at[band, :], out.at[slot, band, :], sem)
            copy.start()
            copies.append(copy)
    for copy in copies:
        copy.wait()


def own_kernel(
    info_ref, tiles_ref, pair_energy_ref, energy_ref, amps_ref, domain, half, mirror_half,
    residual_out, updated_out, other_ref, residual_buf, updated_buf, sems,
):
    energies = (info_ref, tiles_ref, pair_energy_ref, energy_ref)
    slot = info_ref[2]
    for step, band in enumerate(denominators_of(*energies, 1 - slot)):
        other_ref[pl.ds(step * V, V), :] = band
    bands = denominators_of(*energies, slot)

    def residual_of(band):
        return lax.dot_general(
            half[band, :], domain[...], ACROSS, preferred_element_type=jnp.float32
        ) + lax.dot_general(domain[band, :], mirror_half[...], ACROSS, preferred_element_type=jnp.float32)

    write_pair(
        slot, lambda step: bands[step], residual_of, amps_ref,
        residual_out, updated_out, residual_buf, updated_buf, sems,
    )


def other_kernel(
    place_ref, amps_ref, received_ref, denominators_ref, residual_in, updated_in,
    residual_out, updated_out, residual_buf, updated_buf, sems,
):
    write_pair(
        1 - scalar_of(place_ref[2:3]),
        lambda step: denominators_ref[pl.ds(step * V, V), :],
        lambda band: received_ref[band, :].astype(jnp.float32),
        amps_ref, residual_out, updated_out, residual_buf, updated_buf, sems,
    )


def whole(space=VMEM):
    return pl.BlockSpec(memory_space=space)


def shards(amplitudes, factors, tiles, mirror, pair_energy, virt_energy):
    f32, bf16 = jnp.float32, jnp.bfloat16
    sel = jnp.where(lax.axis_index("xa") == 0, 0, 1 - (mirror[0] & 1))
    info = jnp.stack([lax.axis_index(a) for a in ("u", "c")] + [sel, lax.axis_index("y")]).astype(jnp.int32)
    place = jnp.broadcast_to(info.astype(f32)[:, None], (4, V))
    tiles_t = tiles.T

    spread = pl.pallas_call(
        spread_kernel,
        out_shape=jax.ShapeDtypeStruct((NU, ROWS * MSG1, V), bf16),
        in_specs=[whole(pltpu.MemorySpace.HBM), whole(pltpu.MemorySpace.HBM)],
        out_specs=whole(),
        scratch_shapes=[
            pltpu.SMEM(tiles_t.shape, jnp.int32),
            pltpu.VMEM(factors.shape, bf16),
            pltpu.VMEM(((NQ * NT + 1) * ROWS, HALF), f32),
            pltpu.VMEM((ROWS * MSG1, V), f32),
            pltpu.SemaphoreType.DMA((3,)),
        ],
        compiler_params=pltpu.CompilerParams(vmem_limit_bytes=60 * 1024 * 1024),
        name="spread",
    )(tiles_t, factors)
    held = lax.all_to_all(spread.reshape(SOURCES, MSG1 // 2, 2, V), ("u", "b", "xa", "xb"), 0, 0, tiled=True)
    theirs = lax.ppermute(held, "c", [(1, 0), (0, 1)])
    going = lax.dynamic_index_in_dim(amplitudes, 1 - sel, 0, keepdims=False)
    opposite = [(1, 0), (0, 1)]
    mirror_amps = lax.ppermute(going, "xa", opposite)

    held = held.reshape(HELD, V)
    table = pl.pallas_call(
        table_kernel,
        out_shape=jax.ShapeDtypeStruct((GROUP, V), jnp.int32),
        in_specs=[whole(), whole()],
        out_specs=whole(),
        compiler_params=PARAMS,
        name="table",
    )(place, held)
    selected = pl.pallas_call(
        select_kernel,
        out_shape=jax.ShapeDtypeStruct((PLANE * MSG2, V), bf16),
        in_specs=[whole()] * 4,
        out_specs=whole(),
        scratch_shapes=[
            pltpu.VMEM((NC * HELD + 8, V), f32),
            pltpu.VMEM((PLANE * MSG2, V), f32),
            pltpu.SMEM((GROUP, V), jnp.int32),
            pltpu.SemaphoreType.DMA,
        ],
        compiler_params=PARAMS,
        name="select",
    )(place, table, held, theirs.reshape(HELD, V))
    selected, mirror_amps = lax.optimization_barrier((selected, mirror_amps))
    blocks = lax.all_to_all(
        selected.reshape(PLANE, MSG2 // 2, 2, V), ("xb", "xa", "y", "b"), 0, 0, tiled=True
    )

    wide_half = jax.ShapeDtypeStruct((WIDTH, NQ * WIDTH), bf16)
    sent, domain, half, mirror_half = pl.pallas_call(
        ladder_kernel,
        out_shape=(jax.ShapeDtypeStruct((WIDTH, WIDTH), bf16), wide_half, wide_half, wide_half),
        in_specs=[whole()] * 4,
        out_specs=(whole(),) * 4,
        scratch_shapes=[pltpu.VMEM((PLANE * MSG2 + 24, V), f32)],
        compiler_params=PARAMS,
        name="ladder",
    )(place, amplitudes, mirror_amps, blocks.reshape(PLANE * MSG2, V))
    received = lax.ppermute(sent, "xa", opposite)

    energies = virt_energy.reshape(NT, V)
    outs = (
        jax.ShapeDtypeStruct(amplitudes.shape, f32),
        jax.ShapeDtypeStruct(amplitudes.shape, bf16),
    )
    buffers = [
        pltpu.VMEM((WIDTH, WIDTH), f32),
        pltpu.VMEM((WIDTH, WIDTH), bf16),
        pltpu.SemaphoreType.DMA((2, K)),
    ]
    residual, updated, denominators = pl.pallas_call(
        own_kernel,
        out_shape=outs + (jax.ShapeDtypeStruct((WIDTH, WIDTH), f32),),
        in_specs=[whole(SMEM)] * 3 + [whole()] * 5,
        out_specs=(whole(pl.ANY), whole(pl.ANY), whole()),
        scratch_shapes=buffers,
        cost_estimate=pl.CostEstimate(flops=8 * WIDTH**3, bytes_accessed=10 * WIDTH**2, transcendentals=0),
        compiler_params=PARAMS,
        name="own",
    )(info, tiles_t, pair_energy, energies, amplitudes, domain, half, mirror_half)
    residual, updated = pl.pallas_call(
        other_kernel,
        out_shape=outs,
        in_specs=[whole(), whole(), whole(), whole(), whole(pl.ANY), whole(pl.ANY)],
        out_specs=(whole(pl.ANY),) * 2,
        scratch_shapes=buffers,
        input_output_aliases={4: 0, 5: 1},
        cost_estimate=pl.CostEstimate(flops=4 * WIDTH**2, bytes_accessed=10 * WIDTH**2, transcendentals=0),
        compiler_params=PARAMS,
        name="other",
    )(place, amplitudes, received, denominators, residual, updated)
    return (residual, updated)


def solution(mesh):
    fine = Mesh(mesh.devices.reshape(2, NX // 2, NU, NB, NC, NY), ("xa", "xb", "u", "b", "c", "y"))
    pairs = ("xa", "xb", "u", "b", "c")
    return jax.shard_map(
        shards,
        mesh=fine,
        in_specs=(
            P(pairs + ("y",), None, None),
            P(None, None, "y", pairs),
            P(pairs, None),
            P(pairs + ("y",)),
            P(pairs + ("y",)),
            P(),
        ),
        out_specs=(P(pairs + ("y",), None, None), P(pairs + ("y",), None, None)),
        check_vma=False,
    )
```

```python
import jax
import jax.numpy as jnp
from jax import lax
from jax.experimental import pallas as pl
from jax.experimental.pallas import tpu as pltpu
from jax.sharding import Mesh, PartitionSpec as P

V = 128
K = 3
NX, NU, NB, NC, NY = 4, 2, 4, 2, 8
NT = 32
NQ = 2
HALF = V // 2
GROUP = 16
WIDTH = K * V
ROWS = NX * NB
SOURCES = NU * ROWS
PLANE = ROWS * NY
MSG1 = NT + 2
HELD = SOURCES * MSG1
MSG2 = 2 * K * K
SMEM = pltpu.MemorySpace.SMEM
VMEM = pltpu.MemorySpace.VMEM
PARAMS = pltpu.CompilerParams(vmem_limit_bytes=24 * 1024 * 1024)


def spread_kernel(tiles_hbm, factors_hbm, out_ref, tiles, raw, wide, staged, sems):
    slots = [(row % NB) * NX + row // NB for row in range(ROWS)]
    copies = [pltpu.make_async_copy(tiles_hbm, tiles, sems.at[0])]
    part = NT // 2
    for i in range(2):
        strip = pl.ds(i * part, part)
        copies.append(pltpu.make_async_copy(factors_hbm.at[:, strip], raw.at[:, strip], sems.at[1 + i]))
    for copy in copies:
        copy.start()
    copies[0].wait()
    lane = lax.broadcasted_iota(jnp.int32, (2, V), 1)
    tile_row = jnp.zeros((2, V), jnp.float32)
    for member in range(GROUP):
        for k in range(K):
            tile_row = jnp.where(lane == member * K + k, tiles[k, member].astype(jnp.float32), tile_row)
    for row in range(ROWS):
        staged[pl.ds(slots[row] * MSG1 + NT, 2), :] = tile_row
    for i in range(2):
        copies[1 + i].wait()
        for q in range(NQ):
            first = (q * NT + i * part) * ROWS
            wide[pl.ds(first, part * ROWS), :] = (
                raw[q, pl.ds(i * part, part)].astype(jnp.float32).reshape(part * ROWS, HALF)
            )
        for row in range(ROWS):
            for eight in range(part // 8):
                first = (i * part + eight * 8) * ROWS + row
                sides = [wide[pl.ds(q * NT * ROWS + first, 8, stride=ROWS), :] for q in range(NQ)]
                staged[pl.ds(slots[row] * MSG1 + i * part + eight * 8, 8), :] = jnp.concatenate(sides, axis=1)
    packed = staged[...].astype(jnp.bfloat16)
    for u in range(NU):
        out_ref[u] = packed


def scalar_of(row):
    return jnp.max(row).astype(jnp.int32)


def table_kernel(place_ref, held_ref, out_ref):
    which = lax.rem(lax.broadcasted_iota(jnp.int32, (1, V), 1), K)
    start = pl.multiple_of(scalar_of(place_ref[0:1]) * (ROWS * MSG1), 16)
    for group in range(GROUP // 2):
        row = (group % NB * NX + group // NB) * MSG1 + NT
        block = held_ref[pl.ds(pl.multiple_of(start + row // 16 * 16, 16), 16), :].astype(jnp.float32)
        named = block[row % 16 : row % 16 + 1].astype(jnp.int32)
        strip = ((named >> 2) & 1) * ROWS + (named & (NB - 1)) * NX + (named >> 3)
        for k in range(K):
            turned = [named if l == k else pltpu.roll(named, (l - k) % V, 1) for l in range(K)]
            row_tile = jnp.where(which == 0, turned[0], jnp.where(which == 1, turned[1], turned[2]))
            out_ref[pl.ds(group * K + k, 1), :] = 2 * MSG1 * strip + 2 * row_tile


def select_kernel(place_ref, table_ref, mine_ref, theirs_ref, out_ref, wide, staged, table, sem):
    copy = pltpu.make_async_copy(table_ref, table, sem)
    copy.start()
    core = scalar_of(place_ref[1:2])
    wide[pl.ds(core, HELD, stride=2), :] = mine_ref[...].astype(jnp.float32)
    wide[pl.ds(1 - core, HELD, stride=2), :] = theirs_ref[...].astype(jnp.float32)
    copy.wait()

    def one_group(group, carry):
        first = (group // NB * (NX // 2 * NY * NB) + group % NB) * MSG2
        for parity in range(2):
            for y in range(NY):
                member = 2 * y + parity
                base = first + (parity * NY + y) * NB * MSG2
                for l in range(K):
                    for k in range(K):
                        staged[pl.ds(base + (l * K + k) * 2, 2), :] = wide[
                            pl.ds(pl.multiple_of(table[group * K + k, member * K + l], 2), 2), :
                        ]
        return carry

    lax.fori_loop(0, GROUP // 2, one_group, 0)
    out_ref[...] = staged[...].astype(jnp.bfloat16)


ACROSS = (((1,), (1,)), ((), ()))


def ladder_kernel(place_ref, amps_ref, mirror_amps_ref, blocks_ref, sent_ref, domain, half, mirror_half, wide):
    run = NB * MSG2
    for x in range(NX):
        for y in range(0, NY, 2):
            place = x % 2 * (NX // 2) + x // 2
            chunk = blocks_ref[pl.ds((place * NY + y) * run, 2 * run), :].astype(jnp.float32)
            wide[pl.ds((y * NX + x) * run, run), :] = chunk[:run]
            wide[pl.ds(((y + 1) * NX + x) * run, run), :] = chunk[run:]
    left = lax.broadcasted_iota(jnp.int32, (ROWS, V), 1) < HALF
    for y in range(NY):
        for l in range(K):
            for k in range(K):
                first = y * ROWS * MSG2 + (l * K + k) * 2
                sides = [wide[pl.ds(first + h, ROWS, stride=MSG2), :] for h in range(2)]
                rows = pl.ds(k * V + y * ROWS, ROWS)
                for q in range(NQ):
                    block = jnp.where(
                        left,
                        sides[0] if q == 0 else pltpu.roll(sides[0], HALF, 1),
                        sides[1] if q == 1 else pltpu.roll(sides[1], HALF, 1),
                    )
                    domain[rows, pl.ds(q * WIDTH + l * V, V)] = block.astype(jnp.bfloat16)
    own = amps_ref[scalar_of(place_ref[2:3])]
    both = jnp.concatenate([own, mirror_amps_ref[...]], axis=1)
    for q in range(NQ):
        columns = pl.ds(q * WIDTH, WIDTH)
        halves = jnp.dot(domain[:, columns], both, preferred_element_type=jnp.float32).astype(jnp.bfloat16)
        half[:, columns] = halves[:, :WIDTH]
        mirror_half[:, columns] = halves[:, WIDTH:]
    sent_ref[...] = (
        lax.dot_general(domain[...], half[...], ACROSS, preferred_element_type=jnp.float32)
        + lax.dot_general(mirror_half[...], domain[...], ACROSS, preferred_element_type=jnp.float32)
    ).astype(jnp.bfloat16)


def denominators_of(info_ref, tiles_ref, pair_energy_ref, energy_ref, slot):
    member = 2 * info_ref[3] + slot
    rows = [energy_ref[pl.ds(tiles_ref[k, member], 1), :] for k in range(K)]
    across = jnp.concatenate(rows, axis=1)
    bands = []
    for row in rows:
        down = jnp.transpose(jnp.broadcast_to(row, (V, V)))
        bands.append(jnp.concatenate([down] * K, axis=1) + across - pair_energy_ref[slot])
    return bands


def write_pair(slot, denominator_of, residual_of, amps_ref, residual_out, updated_out, residual_buf, updated_buf, sems):
    copies = []
    for step in range(K):
        band = pl.ds(step * V, V)
        residual = residual_of(band)
        residual_buf[band, :] = residual
        updated_buf[band, :] = (
            amps_ref[slot, band, :].astype(jnp.float32) - residual / denominator_of(step)
        ).astype(jnp.bfloat16)
        for buf, out, sem in (
            (residual_buf, residual_out, sems.at[0, step]),
            (updated_buf, updated_out, sems.at[1, step]),
        ):
            copy = pltpu.make_async_copy(buf.at[band, :], out.at[slot, band, :], sem)
            copy.start()
            copies.append(copy)
    for copy in copies:
        copy.wait()


def own_kernel(
    info_ref, tiles_ref, pair_energy_ref, energy_ref, amps_ref, domain, half, mirror_half,
    residual_out, updated_out, other_ref, residual_buf, updated_buf, sems,
):
    energies = (info_ref, tiles_ref, pair_energy_ref, energy_ref)
    slot = info_ref[2]
    for step, band in enumerate(denominators_of(*energies, 1 - slot)):
        other_ref[pl.ds(step * V, V), :] = band
    bands = denominators_of(*energies, slot)

    def residual_of(band):
        return lax.dot_general(
            half[band, :], domain[...], ACROSS, preferred_element_type=jnp.float32
        ) + lax.dot_general(domain[band, :], mirror_half[...], ACROSS, preferred_element_type=jnp.float32)

    write_pair(
        slot, lambda step: bands[step], residual_of, amps_ref,
        residual_out, updated_out, residual_buf, updated_buf, sems,
    )


def other_kernel(
    place_ref, amps_ref, received_ref, denominators_ref, residual_in, updated_in,
    residual_out, updated_out, residual_buf, updated_buf, sems,
):
    write_pair(
        1 - scalar_of(place_ref[2:3]),
        lambda step: denominators_ref[pl.ds(step * V, V), :],
        lambda band: received_ref[band, :].astype(jnp.float32),
        amps_ref, residual_out, updated_out, residual_buf, updated_buf, sems,
    )


def whole(space=VMEM):
    return pl.BlockSpec(memory_space=space)


def shards(amplitudes, factors, tiles, mirror, pair_energy, virt_energy):
    f32, bf16 = jnp.float32, jnp.bfloat16
    sel = jnp.where(lax.axis_index("xa") == 0, 0, 1 - (mirror[0] & 1))
    info = jnp.stack([lax.axis_index(a) for a in ("u", "c")] + [sel, lax.axis_index("y")]).astype(jnp.int32)
    place = jnp.broadcast_to(info.astype(f32)[:, None], (4, V))
    tiles_t = tiles.T

    spread = pl.pallas_call(
        spread_kernel,
        out_shape=jax.ShapeDtypeStruct((NU, ROWS * MSG1, V), bf16),
        in_specs=[whole(pltpu.MemorySpace.HBM), whole(pltpu.MemorySpace.HBM)],
        out_specs=whole(),
        scratch_shapes=[
            pltpu.SMEM(tiles_t.shape, jnp.int32),
            pltpu.VMEM(factors.shape, bf16),
            pltpu.VMEM(((NQ * NT + 1) * ROWS, HALF), f32),
            pltpu.VMEM((ROWS * MSG1, V), f32),
            pltpu.SemaphoreType.DMA((3,)),
        ],
        compiler_params=pltpu.CompilerParams(vmem_limit_bytes=60 * 1024 * 1024),
        name="spread",
    )(tiles_t, factors)
    held = lax.all_to_all(spread.reshape(SOURCES, MSG1 // 2, 2, V), ("u", "b", "xa", "xb"), 0, 0, tiled=True)
    theirs = lax.ppermute(held, "c", [(1, 0), (0, 1)])
    going = lax.dynamic_index_in_dim(amplitudes, 1 - sel, 0, keepdims=False)
    opposite = [(1, 0), (0, 1)]
    mirror_amps = lax.ppermute(going, "xa", opposite)

    held = held.reshape(HELD, V)
    table = pl.pallas_call(
        table_kernel,
        out_shape=jax.ShapeDtypeStruct((GROUP // 2 * K, V), jnp.int32),
        in_specs=[whole(), whole()],
        out_specs=whole(),
        compiler_params=PARAMS,
        name="table",
    )(place, held)
    selected = pl.pallas_call(
        select_kernel,
        out_shape=jax.ShapeDtypeStruct((PLANE * MSG2, V), bf16),
        in_specs=[whole()] * 4,
        out_specs=whole(),
        scratch_shapes=[
            pltpu.VMEM((NC * HELD + 8, V), f32),
            pltpu.VMEM((PLANE * MSG2, V), f32),
            pltpu.SMEM((GROUP // 2 * K, V), jnp.int32),
            pltpu.SemaphoreType.DMA,
        ],
        compiler_params=PARAMS,
        name="select",
    )(place, table, held, theirs.reshape(HELD, V))
    selected, mirror_amps = lax.optimization_barrier((selected, mirror_amps))
    blocks = lax.all_to_all(
        selected.reshape(PLANE, MSG2 // 2, 2, V), ("xb", "xa", "y", "b"), 0, 0, tiled=True
    )

    wide_half = jax.ShapeDtypeStruct((WIDTH, NQ * WIDTH), bf16)
    sent, domain, half, mirror_half = pl.pallas_call(
        ladder_kernel,
        out_shape=(jax.ShapeDtypeStruct((WIDTH, WIDTH), bf16), wide_half, wide_half, wide_half),
        in_specs=[whole()] * 4,
        out_specs=(whole(),) * 4,
        scratch_shapes=[pltpu.VMEM((PLANE * MSG2 + 24, V), f32)],
        compiler_params=PARAMS,
        name="ladder",
    )(place, amplitudes, mirror_amps, blocks.reshape(PLANE * MSG2, V))
    received = lax.ppermute(sent, "xa", opposite)

    energies = virt_energy.reshape(NT, V)
    outs = (
        jax.ShapeDtypeStruct(amplitudes.shape, f32),
        jax.ShapeDtypeStruct(amplitudes.shape, bf16),
    )
    buffers = [
        pltpu.VMEM((WIDTH, WIDTH), f32),
        pltpu.VMEM((WIDTH, WIDTH), bf16),
        pltpu.SemaphoreType.DMA((2, K)),
    ]
    residual, updated, denominators = pl.pallas_call(
        own_kernel,
        out_shape=outs + (jax.ShapeDtypeStruct((WIDTH, WIDTH), f32),),
        in_specs=[whole(SMEM)] * 3 + [whole()] * 5,
        out_specs=(whole(pl.ANY), whole(pl.ANY), whole()),
        scratch_shapes=buffers,
        cost_estimate=pl.CostEstimate(flops=8 * WIDTH**3, bytes_accessed=10 * WIDTH**2, transcendentals=0),
        compiler_params=PARAMS,
        name="own",
    )(info, tiles_t, pair_energy, energies, amplitudes, domain, half, mirror_half)
    residual, updated = pl.pallas_call(
        other_kernel,
        out_shape=outs,
        in_specs=[whole(), whole(), whole(), whole(), whole(pl.ANY), whole(pl.ANY)],
        out_specs=(whole(pl.ANY),) * 2,
        scratch_shapes=buffers,
        input_output_aliases={4: 0, 5: 1},
        cost_estimate=pl.CostEstimate(flops=4 * WIDTH**2, bytes_accessed=10 * WIDTH**2, transcendentals=0),
        compiler_params=PARAMS,
        name="other",
    )(place, amplitudes, received, denominators, residual, updated)
    return (residual, updated)


def solution(mesh):
    fine = Mesh(mesh.devices.reshape(2, NX // 2, NU, NB, NC, NY), ("xa", "xb", "u", "b", "c", "y"))
    pairs = ("xa", "xb", "u", "b", "c")
    return jax.shard_map(
        shards,
        mesh=fine,
        in_specs=(
            P(pairs + ("y",), None, None),
            P(None, None, "y", pairs),
            P(pairs, None),
            P(pairs + ("y",)),
            P(pairs + ("y",)),
            P(),
        ),
        out_specs=(P(pairs + ("y",), None, None), P(pairs + ("y",), None, None)),
        check_vma=False,
    )
```

```python
import jax
import jax.numpy as jnp
from jax import lax
from jax.experimental import pallas as pl
from jax.experimental.pallas import tpu as pltpu
from jax.sharding import Mesh, PartitionSpec as P

V = 128
K = 3
NX, NU, NB, NC, NY = 4, 2, 4, 2, 8
NT = 32
NQ = 2
HALF = V // 2
GROUP = 16
WIDTH = K * V
ROWS = NX * NB
SOURCES = NU * ROWS
PLANE = ROWS * NY
MSG1 = NT + 2
HELD = SOURCES * MSG1
MSG2 = 2 * K * K
SMEM = pltpu.MemorySpace.SMEM
VMEM = pltpu.MemorySpace.VMEM
PARAMS = pltpu.CompilerParams(vmem_limit_bytes=24 * 1024 * 1024)


def spread_kernel(tiles_hbm, factors_hbm, out_ref, tiles, raw, wide, staged, sems):
    slots = [(row % NB) * NX + row // NB for row in range(ROWS)]
    copies = [pltpu.make_async_copy(tiles_hbm, tiles, sems.at[0])]
    part = NT // 2
    for i in range(2):
        strip = pl.ds(i * part, part)
        copies.append(pltpu.make_async_copy(factors_hbm.at[:, strip], raw.at[:, strip], sems.at[1 + i]))
    for copy in copies:
        copy.start()
    copies[0].wait()
    lane = lax.broadcasted_iota(jnp.int32, (2, V), 1)
    tile_row = jnp.zeros((2, V), jnp.float32)
    for member in range(GROUP):
        for k in range(K):
            tile_row = jnp.where(lane == member * K + k, tiles[k, member].astype(jnp.float32), tile_row)
    for row in range(ROWS):
        staged[pl.ds(slots[row] * MSG1 + NT, 2), :] = tile_row
    for i in range(2):
        copies[1 + i].wait()
        for q in range(NQ):
            first = (q * NT + i * part) * ROWS
            wide[pl.ds(first, part * ROWS), :] = (
                raw[q, pl.ds(i * part, part)].astype(jnp.float32).reshape(part * ROWS, HALF)
            )
        for row in range(ROWS):
            for eight in range(part // 8):
                first = (i * part + eight * 8) * ROWS + row
                sides = [wide[pl.ds(q * NT * ROWS + first, 8, stride=ROWS), :] for q in range(NQ)]
                staged[pl.ds(slots[row] * MSG1 + i * part + eight * 8, 8), :] = jnp.concatenate(sides, axis=1)
    packed = staged[...].astype(jnp.bfloat16)
    for u in range(NU):
        out_ref[u] = packed


def scalar_of(row):
    return jnp.max(row).astype(jnp.int32)


def table_kernel(place_ref, held_ref, out_ref):
    which = lax.rem(lax.broadcasted_iota(jnp.int32, (1, V), 1), K)
    start = pl.multiple_of(scalar_of(place_ref[0:1]) * (ROWS * MSG1), 16)
    for group in range(GROUP // 2):
        row = (group % NB * NX + group // NB) * MSG1 + NT
        block = held_ref[pl.ds(pl.multiple_of(start + row // 16 * 16, 16), 16), :].astype(jnp.float32)
        named = block[row % 16 : row % 16 + 1].astype(jnp.int32)
        strip = ((named >> 2) & 1) * ROWS + (named & (NB - 1)) * NX + (named >> 3)
        for k in range(K):
            turned = [named if l == k else pltpu.roll(named, (l - k) % V, 1) for l in range(K)]
            row_tile = jnp.where(which == 0, turned[0], jnp.where(which == 1, turned[1], turned[2]))
            out_ref[pl.ds(group * K + k, 1), :] = 2 * MSG1 * strip + 2 * row_tile


def select_kernel(place_ref, table_ref, mine_ref, theirs_ref, out_ref, wide, staged, table, sem):
    copy = pltpu.make_async_copy(table_ref, table, sem)
    copy.start()
    core = scalar_of(place_ref[1:2])
    wide[pl.ds(core, HELD, stride=2), :] = mine_ref[...].astype(jnp.float32)
    wide[pl.ds(1 - core, HELD, stride=2), :] = theirs_ref[...].astype(jnp.float32)
    copy.wait()

    def one_group(group, carry):
        first = (group // NB * (NX // 2 * NY * NB) + group % NB) * MSG2
        for parity in range(2):
            for y in range(NY):
                member = 2 * y + parity
                base = first + (parity * NY + y) * NB * MSG2
                for l in range(K):
                    for k in range(K):
                        staged[pl.ds(base + (l * K + k) * 2, 2), :] = wide[
                            pl.ds(pl.multiple_of(table[group * K + k, member * K + l], 2), 2), :
                        ]
        return carry

    lax.fori_loop(0, GROUP // 2, one_group, 0)
    out_ref[...] = staged[...].astype(jnp.bfloat16)


ACROSS = (((1,), (1,)), ((), ()))


def ladder_kernel(place_ref, amps_ref, mirror_amps_ref, blocks_ref, sent_ref, domain, half, mirror_half, wide):
    run = NB * MSG2
    for x in range(NX):
        for y in range(0, NY, 2):
            place = x % 2 * (NX // 2) + x // 2
            chunk = blocks_ref[pl.ds((place * NY + y) * run, 2 * run), :].astype(jnp.float32)
            wide[pl.ds((y * NX + x) * run, run), :] = chunk[:run]
            wide[pl.ds(((y + 1) * NX + x) * run, run), :] = chunk[run:]
    left = lax.broadcasted_iota(jnp.int32, (ROWS, V), 1) < HALF
    for y in range(NY):
        for l in range(K):
            for k in range(K):
                first = y * ROWS * MSG2 + (l * K + k) * 2
                sides = [wide[pl.ds(first + h, ROWS, stride=MSG2), :] for h in range(2)]
                rows = pl.ds(k * V + y * ROWS, ROWS)
                for q in range(NQ):
                    block = jnp.where(
                        left,
                        sides[0] if q == 0 else pltpu.roll(sides[0], HALF, 1),
                        sides[1] if q == 1 else pltpu.roll(sides[1], HALF, 1),
                    )
                    domain[rows, pl.ds(q * WIDTH + l * V, V)] = block.astype(jnp.bfloat16)
    own = amps_ref[scalar_of(place_ref[2:3])]
    both = jnp.concatenate([own, mirror_amps_ref[...]], axis=1)
    for q in range(NQ):
        columns = pl.ds(q * WIDTH, WIDTH)
        halves = jnp.dot(domain[:, columns], both, preferred_element_type=jnp.float32).astype(jnp.bfloat16)
        half[:, columns] = halves[:, :WIDTH]
        mirror_half[:, columns] = halves[:, WIDTH:]
    sent_ref[...] = (
        lax.dot_general(domain[...], half[...], ACROSS, preferred_element_type=jnp.float32)
        + lax.dot_general(mirror_half[...], domain[...], ACROSS, preferred_element_type=jnp.float32)
    ).astype(jnp.bfloat16)


def denominators_of(info_ref, tiles_ref, pair_energy_ref, energy_ref, slot):
    member = 2 * info_ref[3] + slot
    rows = [energy_ref[pl.ds(tiles_ref[k, member], 1), :] for k in range(K)]
    across = jnp.concatenate(rows, axis=1)
    bands = []
    for row in rows:
        down = jnp.transpose(jnp.broadcast_to(row, (V, V)))
        bands.append(jnp.concatenate([down] * K, axis=1) + across - pair_energy_ref[slot])
    return bands


def write_pair(slot, denominator_of, residual_of, amps_ref, residual_out, updated_out, residual_buf, updated_buf, sems):
    copies = []

    def send(buf, out, band, sem):
        copies.append(pltpu.make_async_copy(buf.at[band, :], out.at[slot, band, :], sem))
        copies[-1].start()

    bands = [pl.ds(step * V, V) for step in range(K)]
    for step, band in enumerate(bands):
        residual_buf[band, :] = residual_of(band)
        send(residual_buf, residual_out, band, sems.at[0, step])
    for step, band in enumerate(bands):
        change = residual_buf[band, :] / denominator_of(step)
        updated_buf[band, :] = (amps_ref[slot, band, :].astype(jnp.float32) - change).astype(jnp.bfloat16)
        send(updated_buf, updated_out, band, sems.at[1, step])
    for copy in copies:
        copy.wait()


def own_kernel(
    info_ref, tiles_ref, pair_energy_ref, energy_ref, amps_ref, domain, half, mirror_half,
    residual_out, updated_out, other_ref, residual_buf, updated_buf, sems,
):
    energies = (info_ref, tiles_ref, pair_energy_ref, energy_ref)
    slot = info_ref[2]
    for step, band in enumerate(denominators_of(*energies, 1 - slot)):
        other_ref[pl.ds(step * V, V), :] = band
    bands = denominators_of(*energies, slot)

    def residual_of(band):
        return lax.dot_general(
            half[band, :], domain[...], ACROSS, preferred_element_type=jnp.float32
        ) + lax.dot_general(domain[band, :], mirror_half[...], ACROSS, preferred_element_type=jnp.float32)

    write_pair(
        slot, lambda step: bands[step], residual_of, amps_ref,
        residual_out, updated_out, residual_buf, updated_buf, sems,
    )


def other_kernel(
    place_ref, amps_ref, received_ref, denominators_ref, residual_in, updated_in,
    residual_out, updated_out, residual_buf, updated_buf, sems,
):
    write_pair(
        1 - scalar_of(place_ref[2:3]),
        lambda step: denominators_ref[pl.ds(step * V, V), :],
        lambda band: received_ref[band, :].astype(jnp.float32),
        amps_ref, residual_out, updated_out, residual_buf, updated_buf, sems,
    )


def whole(space=VMEM):
    return pl.BlockSpec(memory_space=space)


def shards(amplitudes, factors, tiles, mirror, pair_energy, virt_energy):
    f32, bf16 = jnp.float32, jnp.bfloat16
    sel = jnp.where(lax.axis_index("xa") == 0, 0, 1 - (mirror[0] & 1))
    info = jnp.stack([lax.axis_index(a) for a in ("u", "c")] + [sel, lax.axis_index("y")]).astype(jnp.int32)
    place = jnp.broadcast_to(info.astype(f32)[:, None], (4, V))
    tiles_t = tiles.T

    spread = pl.pallas_call(
        spread_kernel,
        out_shape=jax.ShapeDtypeStruct((NU, ROWS * MSG1, V), bf16),
        in_specs=[whole(pltpu.MemorySpace.HBM), whole(pltpu.MemorySpace.HBM)],
        out_specs=whole(),
        scratch_shapes=[
            pltpu.SMEM(tiles_t.shape, jnp.int32),
            pltpu.VMEM(factors.shape, bf16),
            pltpu.VMEM(((NQ * NT + 1) * ROWS, HALF), f32),
            pltpu.VMEM((ROWS * MSG1, V), f32),
            pltpu.SemaphoreType.DMA((3,)),
        ],
        compiler_params=pltpu.CompilerParams(vmem_limit_bytes=60 * 1024 * 1024),
        name="spread",
    )(tiles_t, factors)
    held = lax.all_to_all(spread.reshape(SOURCES, MSG1 // 2, 2, V), ("u", "b", "xa", "xb"), 0, 0, tiled=True)
    theirs = lax.ppermute(held, "c", [(1, 0), (0, 1)])
    going = lax.dynamic_index_in_dim(amplitudes, 1 - sel, 0, keepdims=False)
    opposite = [(1, 0), (0, 1)]
    mirror_amps = lax.ppermute(going, "xa", opposite)

    held = held.reshape(HELD, V)
    table = pl.pallas_call(
        table_kernel,
        out_shape=jax.ShapeDtypeStruct((GROUP // 2 * K, V), jnp.int32),
        in_specs=[whole(), whole()],
        out_specs=whole(),
        compiler_params=PARAMS,
        name="table",
    )(place, held)
    selected = pl.pallas_call(
        select_kernel,
        out_shape=jax.ShapeDtypeStruct((PLANE * MSG2, V), bf16),
        in_specs=[whole()] * 4,
        out_specs=whole(),
        scratch_shapes=[
            pltpu.VMEM((NC * HELD + 8, V), f32),
            pltpu.VMEM((PLANE * MSG2, V), f32),
            pltpu.SMEM((GROUP // 2 * K, V), jnp.int32),
            pltpu.SemaphoreType.DMA,
        ],
        compiler_params=PARAMS,
        name="select",
    )(place, table, held, theirs.reshape(HELD, V))
    selected, mirror_amps = lax.optimization_barrier((selected, mirror_amps))
    blocks = lax.all_to_all(
        selected.reshape(PLANE, MSG2 // 2, 2, V), ("xb", "xa", "y", "b"), 0, 0, tiled=True
    )

    wide_half = jax.ShapeDtypeStruct((WIDTH, NQ * WIDTH), bf16)
    sent, domain, half, mirror_half = pl.pallas_call(
        ladder_kernel,
        out_shape=(jax.ShapeDtypeStruct((WIDTH, WIDTH), bf16), wide_half, wide_half, wide_half),
        in_specs=[whole()] * 4,
        out_specs=(whole(),) * 4,
        scratch_shapes=[pltpu.VMEM((PLANE * MSG2 + 24, V), f32)],
        compiler_params=PARAMS,
        name="ladder",
    )(place, amplitudes, mirror_amps, blocks.reshape(PLANE * MSG2, V))
    received = lax.ppermute(sent, "xa", opposite)

    energies = virt_energy.reshape(NT, V)
    outs = (
        jax.ShapeDtypeStruct(amplitudes.shape, f32),
        jax.ShapeDtypeStruct(amplitudes.shape, bf16),
    )
    buffers = [
        pltpu.VMEM((WIDTH, WIDTH), f32),
        pltpu.VMEM((WIDTH, WIDTH), bf16),
        pltpu.SemaphoreType.DMA((2, K)),
    ]
    residual, updated, denominators = pl.pallas_call(
        own_kernel,
        out_shape=outs + (jax.ShapeDtypeStruct((WIDTH, WIDTH), f32),),
        in_specs=[whole(SMEM)] * 3 + [whole()] * 5,
        out_specs=(whole(pl.ANY), whole(pl.ANY), whole()),
        scratch_shapes=buffers,
        cost_estimate=pl.CostEstimate(flops=8 * WIDTH**3, bytes_accessed=10 * WIDTH**2, transcendentals=0),
        compiler_params=PARAMS,
        name="own",
    )(info, tiles_t, pair_energy, energies, amplitudes, domain, half, mirror_half)
    residual, updated = pl.pallas_call(
        other_kernel,
        out_shape=outs,
        in_specs=[whole(), whole(), whole(), whole(), whole(pl.ANY), whole(pl.ANY)],
        out_specs=(whole(pl.ANY),) * 2,
        scratch_shapes=buffers,
        input_output_aliases={4: 0, 5: 1},
        cost_estimate=pl.CostEstimate(flops=4 * WIDTH**2, bytes_accessed=10 * WIDTH**2, transcendentals=0),
        compiler_params=PARAMS,
        name="other",
    )(place, amplitudes, received, denominators, residual, updated)
    return (residual, updated)


def solution(mesh):
    fine = Mesh(mesh.devices.reshape(2, NX // 2, NU, NB, NC, NY), ("xa", "xb", "u", "b", "c", "y"))
    pairs = ("xa", "xb", "u", "b", "c")
    return jax.shard_map(
        shards,
        mesh=fine,
        in_specs=(
            P(pairs + ("y",), None, None),
            P(None, None, "y", pairs),
            P(pairs, None),
            P(pairs + ("y",)),
            P(pairs + ("y",)),
            P(),
        ),
        out_specs=(P(pairs + ("y",), None, None), P(pairs + ("y",), None, None)),
        check_vma=False,
    )
```
